32 devices in a mesh: shard: 2 (over x), replica: 16 (over z, y, core).
Axes of the slice: x: 2, y: 2, z: 4, core: 2. Of those that a mesh axis runs over, the one named last changes fastest.
Arguments:
- tokens: bfloat16 [32768, 576], P(('shard', 'replica')), may hold values from -6 to 6
- cotangent: bfloat16 [32768, 576], P(('shard', 'replica')), may hold values from -6 to 6
- lengths: int32 [32, 4], P(('shard', 'replica')), may hold values from 0 to 1024, as said below
- attn_gain: bfloat16 [576], P('shard'), may hold values from 0.5 to 1.5
- w_query: bfloat16 [576, 576], P('shard'), may hold values from -0.25 to 0.25
- key_projection: bfloat16 [576, 192], P('shard'), may hold values from -0.25 to 0.25
- value_projection: bfloat16 [576, 192], P('shard'), may hold values from -0.25 to 0.25
- w_out: bfloat16 [576, 576], P('shard'), may hold values from -1 to 1
- mlp_gain: bfloat16 [576], P('shard'), may hold values from 0.5 to 1.5
- w_gate: bfloat16 [576, 1536], P('shard'), may hold values from -0.25 to 0.25
- w_up: bfloat16 [576, 1536], P('shard'), may hold values from -0.25 to 0.25
- w_down: bfloat16 [1536, 576], P('shard'), may hold values from -0.15625 to 0.15625
Outputs:
- block_out: bfloat16 [32768, 576], P(('shard', 'replica'))
- grad_tokens: bfloat16 [32768, 576], P(('shard', 'replica'))
- grad_attn_gain: float32 [576], P('shard')
- grad_query: float32 [576, 576], P('shard')
- grad_key: float32 [576, 192], P('shard')
- grad_value: float32 [576, 192], P('shard')
- grad_out: float32 [576, 576], P('shard')
- grad_mlp_gain: float32 [576], P('shard')
- grad_gate: float32 [576, 1536], P('shard')
- grad_up: float32 [576, 1536], P('shard')
- grad_down: float32 [1536, 576], P('shard')
The draws below stay inside these ranges and needn't reach their ends.
Inputs may be any that keep to these rules, and one draw needn't show every extreme that they name: `lengths`: each row holds one sequence of 1024 slots; later entries are 0 (empty slots).
All inputs are finite; a program needn't handle non-finite values.
Results may differ from the reference program's by a relative error of at most 0.015.
Values may be sent and summed in bfloat16 or wider, within the bound.
No kernel may reach another device: no remote copies, remote signals or barrier semaphores. Data moves between devices by JAX's collectives and lax.ppermute only.
A program may use at most 192 MiB of HBM per device.

```python
import math
import jax
import jax.numpy as jnp
from jax import lax

MODEL_WIDTH = 576
QUERY_HEADS = 9
KEY_VALUE_HEADS = 3
HEAD_SIZE = 64
FF = 1536
CAP = 1024
MINLEN = 1024
SLOTS = 4
TOKENS = 32768
N_SHARD = 2
N_REPLICA = 16


def draw_lengths(key, part):
    key = jax.random.fold_in(key, 11)
    device_rows = N_SHARD * N_REPLICA
    subkeys = jax.random.split(key, 4)
    shortest = min(MINLEN, CAP)
    single = jax.random.randint(subkeys[0], (device_rows,), shortest, CAP + 1).astype(jnp.int32)
    table = jnp.zeros((device_rows, SLOTS), jnp.int32).at[:, 0].set(single)
    if CAP >= 2 * MINLEN:
        second = jax.random.randint(subkeys[1], (device_rows,), MINLEN, CAP - MINLEN + 1).astype(jnp.int32)
        paired = jnp.zeros((device_rows, SLOTS), jnp.int32).at[:, 0].set(MINLEN).at[:, 1].set(second)
        picked = jax.random.randint(subkeys[2], (device_rows,), 0, 2) == 1
        table = jnp.where(picked[:, None], paired, table)
    chosen = jax.random.randint(subkeys[3], (), 0, device_rows)
    single_row = jnp.zeros((SLOTS,), jnp.int32).at[0].set(CAP)
    table = jnp.where((jnp.arange(device_rows) == chosen)[:, None], single_row[None, :], table)
    return table.astype(jnp.int32)


def steps_of(rng, extent, pieces, low, high):
    factor_of, own = 1.0, jax.random.fold_in(rng, 6)
    for axis_at, shards_of in pieces:
        steps = jnp.exp(jax.random.uniform(jax.random.fold_in(own, axis_at), (shards_of,), jnp.float32, low / len(pieces), high / len(pieces)))
        factor_of = factor_of * jnp.repeat(steps, extent[axis_at] // shards_of).reshape([-1 if axis == axis_at else 1 for axis in range(len(extent))])
    return factor_of


def normal_values(key, extent, spread, bound, pieces=(), held_as=jnp.bfloat16):
    values = jax.random.normal(key, extent, jnp.float32) * spread
    if len(pieces) > 0:
        values = steps_of(key, extent, pieces, -0.22, 0.18) * values
    return jnp.clip(values, min=-bound, max=bound).astype(held_as)


def setup_inputs(seed: int = 0) -> dict:
    arg_keys = jax.random.split(jax.random.key(seed), 13)
    return {
        "tokens": normal_values(arg_keys[0], (TOKENS, MODEL_WIDTH), 1.0, 6.0, ((0, 32),)),
        "cotangent": normal_values(arg_keys[1], (TOKENS, MODEL_WIDTH), 1.0, 6.0, ((0, 32),)),
        "lengths": draw_lengths(jax.random.fold_in(arg_keys[12], 71), 0),
        "attn_gain": jnp.clip(1.0 + 0.1 * jax.random.normal(arg_keys[3], (MODEL_WIDTH,), jnp.float32), 0.5, 1.5).astype(jnp.bfloat16),
        "w_query": normal_values(arg_keys[4], (MODEL_WIDTH, QUERY_HEADS * HEAD_SIZE), MODEL_WIDTH ** -0.5, 0.25, ((0, 2),)),
        "key_projection": normal_values(arg_keys[5], (MODEL_WIDTH, KEY_VALUE_HEADS * HEAD_SIZE), MODEL_WIDTH ** -0.5, 0.25, ((0, 2),)),
        "value_projection": normal_values(arg_keys[6], (MODEL_WIDTH, KEY_VALUE_HEADS * HEAD_SIZE), MODEL_WIDTH ** -0.5, 0.25, ((0, 2),)),
        "w_out": normal_values(arg_keys[7], (QUERY_HEADS * HEAD_SIZE, MODEL_WIDTH), (QUERY_HEADS * HEAD_SIZE // 16) ** -0.5, 1.0, ((0, 2),)),
        "mlp_gain": jnp.clip(1.0 + 0.1 * jax.random.normal(arg_keys[8], (MODEL_WIDTH,), jnp.float32), 0.5, 1.5).astype(jnp.bfloat16),
        "w_gate": normal_values(arg_keys[9], (MODEL_WIDTH, FF), MODEL_WIDTH ** -0.5, 0.25, ((0, 2),)),
        "w_up": normal_values(arg_keys[10], (MODEL_WIDTH, FF), MODEL_WIDTH ** -0.5, 0.25, ((0, 2),)),
        "w_down": normal_values(arg_keys[11], (FF, MODEL_WIDTH), FF ** -0.5, 0.15625, ((0, 2),)),
    }


@jax.custom_vjp
def lower_precision(v):
    return lax.optimization_barrier(v.astype(jnp.bfloat16)).astype(jnp.float32)

@jax.custom_vjp
def lower_precision_back(v):
    return v

def low_keep(v):
    return (lower_precision(v), None)

def low_pass(kept, grad):
    return (grad,)

def back_keep(v):
    return (v, None)

def back_low(kept, grad):
    return (lower_precision(grad),)
lower_precision.defvjp(low_keep, low_pass)
lower_precision_back.defvjp(back_keep, back_low)
EPS = 1e-05
THETA = 100000.0
HIGH_PRECISION = lax.Precision.HIGHEST

def layout(lens_row, count_of_rows):
    seq_ends = jnp.cumsum(lens_row).astype(jnp.int32)
    places = jnp.arange(count_of_rows, dtype=jnp.int32)
    segment = lax.optimization_barrier(jnp.sum((places[:, None] >= seq_ends[None, :]).astype(jnp.int32), axis=1)).astype(jnp.int32)
    starts = (seq_ends - lens_row).astype(jnp.int32)
    slot_ids = jnp.arange(lens_row.shape[0], dtype=jnp.int32)
    in_slot = segment[:, None] == slot_ids[None, :]
    seq_start = lax.optimization_barrier(jnp.sum(jnp.where(in_slot, starts[None, :], 0), axis=1)).astype(jnp.int32)
    seq_start = seq_start + jnp.where(segment == lens_row.shape[0], seq_ends[-1], 0).astype(jnp.int32)
    return (segment, (places - seq_start).astype(jnp.int32), segment < lens_row.shape[0])

def apply_rotation(vector, token_position):
    width = vector.shape[-1]
    half_width = width // 2
    inverse = jnp.exp(jnp.arange(half_width, dtype=jnp.float32) * (-2.0 * math.log(THETA) / width))
    angles = token_position.astype(jnp.float32)[:, None] * inverse[None, :]
    cosine_table = jnp.concatenate([jnp.cos(angles), jnp.cos(angles)], -1)[:, None, :]
    sine_table = jnp.concatenate([jnp.sin(angles), jnp.sin(angles)], -1)[:, None, :]
    turned = jnp.concatenate([-vector[..., half_width:], vector[..., :half_width]], -1)
    return vector * cosine_table + turned * sine_table

def normalize(vector, gain_vec):
    return vector * lax.rsqrt(lax.optimization_barrier(jnp.mean(vector * vector, -1, keepdims=True)) + EPS) * gain_vec

def block_forward(source, lens_row, params):
    gain_one, query_w, key_matrix, value_matrix, out_w, gain_two, gate_w, up_w, down_w = params
    count_of_rows = source.shape[0]
    segment, token_position, valid = layout(lens_row, count_of_rows)
    first_normed_input = lower_precision(normalize(source, gain_one))
    query_heads = lower_precision_back(jnp.dot(first_normed_input, query_w, precision=HIGH_PRECISION)).reshape(count_of_rows, QUERY_HEADS, HEAD_SIZE)
    key_heads = lower_precision_back(jnp.dot(first_normed_input, key_matrix, precision=HIGH_PRECISION)).reshape(count_of_rows, KEY_VALUE_HEADS, HEAD_SIZE)
    value_heads = lower_precision(lower_precision_back(jnp.dot(first_normed_input, value_matrix, precision=HIGH_PRECISION))).reshape(count_of_rows, KEY_VALUE_HEADS, HEAD_SIZE)
    query_heads = lower_precision(apply_rotation(query_heads, token_position)).reshape(count_of_rows, KEY_VALUE_HEADS, QUERY_HEADS // KEY_VALUE_HEADS, HEAD_SIZE)
    key_heads = lower_precision(apply_rotation(key_heads, token_position))
    scores = jnp.einsum('qgha,kga->ghqk', query_heads, key_heads, precision=HIGH_PRECISION) * (1.0 / math.sqrt(HEAD_SIZE))
    scores = lower_precision_back(scores)
    places = jnp.arange(count_of_rows, dtype=jnp.int32)
    allowed = (segment[:, None] == segment[None, :]) & (places[None, :] <= places[:, None])
    scores = jnp.where(allowed[None, None], scores, -1e+30)
    row_max = lax.optimization_barrier(jnp.max(scores, -1, keepdims=True))
    raised = jnp.exp(scores - row_max)
    probability = raised / lax.optimization_barrier(jnp.sum(raised, -1, keepdims=True))
    heads = jnp.einsum('ghqk,kga->qgha', lower_precision(probability), value_heads, precision=HIGH_PRECISION)
    heads = lower_precision(lower_precision_back(heads.reshape(count_of_rows, QUERY_HEADS * HEAD_SIZE)))
    middle = source + lower_precision_back(jnp.dot(heads, out_w, precision=HIGH_PRECISION))
    normed_two = lower_precision(normalize(middle, gain_two))
    gate = lower_precision_back(jnp.dot(normed_two, gate_w, precision=HIGH_PRECISION))
    up_act = lower_precision_back(jnp.dot(normed_two, up_w, precision=HIGH_PRECISION))
    hidden = lower_precision(jax.nn.silu(gate) * up_act)
    result = middle + lower_precision_back(jnp.dot(hidden, down_w, precision=HIGH_PRECISION))
    return result * valid.astype(result.dtype)[:, None]

def reference(tokens, cotangent, lengths, attn_gain, w_query, key_projection, value_projection, w_out, mlp_gain, w_gate, w_up, w_down):
    params = tuple((weight.astype(jnp.float32) for weight in (attn_gain, w_query, key_projection, value_projection, w_out, mlp_gain, w_gate, w_up, w_down)))
    device_rows = lengths.shape[0]
    source = tokens.astype(jnp.float32).reshape(device_rows, CAP, MODEL_WIDTH)
    stepper = jax.checkpoint(block_forward)

    def entire(source_all, params_all):

        def single(packed):
            return stepper(packed[0], packed[1], params_all)
        return lax.map(single, (source_all, lengths))
    output, pull_back = jax.vjp(entire, source, params)
    grad_source, grads = pull_back(cotangent.astype(jnp.float32).reshape(device_rows, CAP, MODEL_WIDTH))
    return (output.reshape(-1, MODEL_WIDTH).astype(jnp.bfloat16), grad_source.reshape(-1, MODEL_WIDTH).astype(jnp.bfloat16), grads[0], grads[1], grads[2], grads[3], grads[4], grads[5], grads[6], grads[7], grads[8])
```

```python
import functools
import math

import jax
import jax.numpy as jnp
import numpy as np
from jax import lax
from jax.experimental import pallas as pl
from jax.experimental.pallas import tpu as pltpu
from jax.sharding import PartitionSpec as P

QUERY_HEADS = 9
KEY_VALUE_HEADS = 3
HEAD_SIZE = 64
HALF = HEAD_SIZE // 2
GROUP = QUERY_HEADS // KEY_VALUE_HEADS
EPS = 1e-05
THETA = 100000.0
BF = jnp.bfloat16
F32 = jnp.float32
BLOCK = 256
VMEM_LIMIT = 56 * 2**20
AXES = ("shard", "replica")


def nn(a, b):
    return lax.dot_general(a, b, (((1,), (0,)), ((), ())), preferred_element_type=F32)


def nt(a, b):
    return lax.dot_general(a, b, (((1,), (1,)), ((), ())), preferred_element_type=F32)


def tn(a, b):
    return lax.dot_general(a, b, (((0,), (0,)), ((), ())), preferred_element_type=F32)


def whole():
    return pl.BlockSpec(memory_space=pltpu.VMEM)


def call(kernel, name, outs, flops, grid=None, in_specs=None, out_specs=None, scratch=()):
    return pl.pallas_call(
        kernel,
        name=name,
        out_shape=outs,
        grid=grid or (),
        in_specs=in_specs,
        out_specs=out_specs,
        scratch_shapes=list(scratch),
        compiler_params=pltpu.CompilerParams(vmem_limit_bytes=VMEM_LIMIT),
        cost_estimate=pl.CostEstimate(flops=flops, bytes_accessed=8 * 2**20, transcendentals=0),
    )


def shape(*dims, dtype=BF):
    return jax.ShapeDtypeStruct(dims, dtype)


def tables(count):
    inverse = np.exp(np.arange(HALF, dtype=np.float32) * np.float32(-2.0 * math.log(THETA) / HEAD_SIZE))
    angles = jnp.arange(count, dtype=jnp.int32).astype(F32)[None, :] * jnp.asarray(inverse)[:, None]
    return jnp.cos(angles), jnp.sin(angles)


def qkv_kernel(x_ref, gain_ref, w_ref, cos_ref, sin_ref, n_ref, q_ref, k_ref, v_ref):
    count = x_ref.shape[1]
    gain = gain_ref[...]
    for at in range(0, count, BLOCK):
        cols = slice(at, at + BLOCK)
        x = x_ref[:, cols].astype(F32)
        r = lax.rsqrt(jnp.mean(x * x, axis=0, keepdims=True) + EPS)
        n_ref[:, cols] = (x * r * gain).astype(BF)
    width_q = q_ref.shape[0]
    width_k = k_ref.shape[0]
    for at in range(0, count, BLOCK):
        cols = slice(at, at + BLOCK)
        y = tn(w_ref[...], n_ref[:, cols])
        c = cos_ref[:, cols]
        s = sin_ref[:, cols]
        for head in range((width_q + width_k) // HEAD_SIZE):
            row = head * HEAD_SIZE
            u1 = y[row : row + HALF]
            u2 = y[row + HALF : row + HEAD_SIZE]
            a = u1 * c - u2 * s
            b = u2 * c + u1 * s
            if row < width_q:
                a = a.astype(BF).astype(F32) * 0.125
                b = b.astype(BF).astype(F32) * 0.125
                q_ref[row : row + HALF, cols] = a.astype(BF)
                q_ref[row + HALF : row + HEAD_SIZE, cols] = b.astype(BF)
            else:
                row -= width_q
                k_ref[row : row + HALF, cols] = a.astype(BF)
                k_ref[row + HALF : row + HEAD_SIZE, cols] = b.astype(BF)
        v_ref[:, cols] = y[width_q + width_k :].astype(BF)


def causal(s, diagonal):
    low = s.shape[0] - diagonal
    rows = lax.broadcasted_iota(jnp.int32, (diagonal, s.shape[1]), 0)
    cols = lax.broadcasted_iota(jnp.int32, (diagonal, s.shape[1]), 1)
    last = jnp.where(rows <= cols, s[low:], -1e30)
    return last if low == 0 else jnp.concatenate([s[:low], last], axis=0)


def attend_kernel(q_ref, k_ref, v_ref, o_ref, lse_ref):
    count = q_ref.shape[1]
    keys = k_ref[...].astype(F32).T.astype(BF)
    for head in range(GROUP):
        rows = slice(head * HEAD_SIZE, (head + 1) * HEAD_SIZE)
        for at in range(0, count, BLOCK):
            end = at + BLOCK
            cols = slice(at, end)
            s = causal(nn(keys[:end], q_ref[rows, cols]), BLOCK)
            top = jnp.max(s, axis=0, keepdims=True)
            p = jnp.exp(s - top)
            total = jnp.sum(p, axis=0, keepdims=True)
            o = nn(v_ref[:, :end], p.astype(BF))
            o_ref[rows, cols] = (o / total).astype(BF)
            lse_ref[0, head : head + 1, cols] = top + jnp.log(total)


def middle_kernel(x_ref, heads_ref, w_ref, gain_ref, mid_ref, n_ref):
    count = x_ref.shape[1]
    gain = gain_ref[...]
    for at in range(0, count, BLOCK):
        cols = slice(at, at + BLOCK)
        m = x_ref[:, cols].astype(F32) + tn(w_ref[...], heads_ref[:, cols])
        r = lax.rsqrt(jnp.mean(m * m, axis=0, keepdims=True) + EPS)
        mid_ref[:, cols] = m
        n_ref[:, cols] = (m * r * gain).astype(BF)


def norm_back(x, gain, grad):
    r = lax.rsqrt(jnp.mean(x * x, axis=0, keepdims=True) + EPS)
    scaled = gain * grad
    dot = jnp.mean(scaled * x, axis=0, keepdims=True)
    return r * scaled - x * (r * r * r * dot)


def mlp_kernel(n_ref, cot_ref, mid_ref, gain_ref, heads_ref, wo_ref, wg_ref, wu_ref, wd_ref,
               gd_ref, gg_ref, gu_ref, out_ref, gmid_ref, gheads_ref, gwo_ref, acc_ref, gn_ref):
    step = pl.program_id(0)
    count = n_ref.shape[1]
    n = n_ref[...]
    cot = cot_ref[...]
    wg, wu, wd = wg_ref[...], wu_ref[...], wd_ref[...]
    gate = tn(wg, n)
    up = tn(wu, n)
    gh = tn(wd, cot)
    sig = 1.0 / (1.0 + jnp.exp(-gate))
    act = gate * sig
    hidden = (act * up).astype(BF)
    gup = (gh * act).astype(BF)
    ggate = (gh * up * (sig * (1.0 + gate * (1.0 - sig)))).astype(BF)
    gd_ref[...] = nt(cot, hidden).astype(BF)
    gg_ref[...] = nt(n, ggate).astype(BF)
    gu_ref[...] = nt(n, gup).astype(BF)
    part = nn(wd, hidden)
    gpart = nn(wg, ggate) + nn(wu, gup)

    @pl.when(step == 0)
    def _():
        acc_ref[...] = part
        gn_ref[...] = gpart

    @pl.when(step > 0)
    def _():
        acc_ref[...] += part
        gn_ref[...] += gpart

    @pl.when(step == pl.num_programs(0) - 1)
    def _():
        gain = gain_ref[...]
        for at in range(0, count, BLOCK):
            cols = slice(at, at + BLOCK)
            mid = mid_ref[:, cols]
            out_ref[:, cols] = (mid + acc_ref[:, cols]).astype(BF)
            gm = cot_ref[:, cols].astype(F32) + norm_back(mid, gain, gn_ref[:, cols])
            gmid_ref[:, cols] = gm
            gheads_ref[:, cols] = nn(wo_ref[...], gm.astype(BF)).astype(BF)
        gwo_ref[...] = nt(heads_ref[...], gmid_ref[...].astype(BF)).astype(BF)


def attend_back_kernel(q_ref, k_ref, v_ref, o_ref, lse_ref, go_ref, cos_ref, sin_ref,
                       gq_ref, gk_ref, gv_ref, dk_ref, dv_ref):
    count = q_ref.shape[1]
    keys = k_ref[...].astype(F32).T.astype(BF)
    values = v_ref[...].astype(F32).T.astype(BF)
    dk_ref[...] = jnp.zeros_like(dk_ref)
    dv_ref[...] = jnp.zeros_like(dv_ref)
    for head in range(GROUP):
        rows = slice(head * HEAD_SIZE, (head + 1) * HEAD_SIZE)
        for at in range(0, count, BLOCK):
            end = at + BLOCK
            cols = slice(at, end)
            q = q_ref[rows, cols]
            go = go_ref[rows, cols]
            delta = jnp.sum(go.astype(F32) * o_ref[rows, cols].astype(F32), axis=0, keepdims=True)
            s = causal(nn(keys[:end], q), BLOCK)
            p = jnp.exp(s - lse_ref[0, head : head + 1, cols])
            ds = (p * (nn(values[:end], go) - delta)).astype(BF)
            dv_ref[:, :end] += nt(go, p.astype(BF))
            dk_ref[:, :end] += nt(q, ds)
            dq = nn(k_ref[:, :end], ds) * 0.125
            c = cos_ref[:, cols]
            sn = sin_ref[:, cols]
            g1, g2 = dq[:HALF], dq[HALF:]
            gq_ref[head * HEAD_SIZE : head * HEAD_SIZE + HALF, cols] = (g1 * c + g2 * sn).astype(BF)
            gq_ref[head * HEAD_SIZE + HALF : (head + 1) * HEAD_SIZE, cols] = (g2 * c - g1 * sn).astype(BF)
    c = cos_ref[...]
    sn = sin_ref[...]
    g1, g2 = dk_ref[:HALF], dk_ref[HALF:]
    gk_ref[:HALF] = (g1 * c + g2 * sn).astype(BF)
    gk_ref[HALF:] = (g2 * c - g1 * sn).astype(BF)
    gv_ref[...] = dv_ref[...].astype(BF)


def weight_kernel(n_ref, gq_ref, gk_ref, gv_ref, out_ref):
    wq = gq_ref.shape[0]
    wk = gk_ref.shape[0]
    n = n_ref[...]
    g = jnp.concatenate([gq_ref[...], gk_ref[...], gv_ref[...]], axis=0)
    out_ref[...] = nt(n, g).astype(BF)


def tokens_kernel(x_ref, gain_ref, w_ref, gq_ref, gk_ref, gv_ref, gmid_ref, out_ref):
    count = x_ref.shape[1]
    gain = gain_ref[...]
    for at in range(0, count, BLOCK):
        cols = slice(at, at + BLOCK)
        g = jnp.concatenate([gq_ref[:, cols], gk_ref[:, cols], gv_ref[:, cols]], axis=0)
        gn = nn(w_ref[...], g)
        x = x_ref[:, cols].astype(F32)
        out_ref[:, cols] = (gmid_ref[:, cols] + norm_back(x, gain, gn)).astype(BF)


class Grid:
    def __init__(self, shards, replicas):
        self.shards, self.replicas = shards, replicas
        self.shard = lax.axis_index("shard")
        self.replica = lax.axis_index("replica")
        self.bits = [1 << i for i in range(1, replicas.bit_length() - 1)]

    def swap(self, a, shard=0, bit=0):
        pairs = []
        for s in range(self.shards):
            for r in range(self.replicas):
                pairs.append((s * self.replicas + r, (s ^ shard) * self.replicas + (r ^ bit)))
        return lax.ppermute(a, AXES, pairs)

    def side(self, bit):
        return (self.replica // bit) % 2


def pick(a, index):
    return lax.dynamic_index_in_dim(a, index, 0, keepdims=False)


def joined(side, mine, other, axis):
    return jnp.where(
        side == 0, jnp.concatenate([mine, other], axis), jnp.concatenate([other, mine], axis)
    )


def gather(grid, own, split, axis):
    side = grid.side(1)
    size = own.shape[split] // 2
    half = lax.dynamic_slice_in_dim(own, side * size, size, split)
    first = grid.swap(half, shard=1)
    second = grid.swap(first, bit=1)
    other = joined(side, first, second, split)
    return joined(grid.shard, own, other, axis)


def add(a, b):
    return (a.astype(F32) + b.astype(F32)).astype(BF)


def total(grid, grads):
    side = grid.side(1)
    a = add(pick(grads, side), grid.swap(pick(grads, 1 - side), bit=1))
    a = add(pick(a, grid.shard), grid.swap(pick(a, 1 - grid.shard), shard=1))
    bits = grid.bits[1:] + grid.bits[:1]
    split = []
    for bit in bits:
        rows = a.shape[0]
        if bit != bits[-1] and rows % 16 == 0:
            two = a.reshape(2, rows // 2, *a.shape[1:])
            mine = grid.side(bit)
            a = add(pick(two, mine), grid.swap(pick(two, 1 - mine), bit=bit))
            split.append(bit)
        else:
            a = add(a, grid.swap(a, bit=bit))
    for bit in reversed(split):
        a = joined(grid.side(bit), a, grid.swap(a, bit=bit), 0)
    other = grid.swap(a, bit=1)
    return jnp.where(side == 0, jnp.stack([a, other]), jnp.stack([other, a]))


def local(shards, replicas, tokens, cotangent, lengths, attn_gain, w_query, key_projection,
          value_projection, w_out, mlp_gain, w_gate, w_up, w_down):
    grid = Grid(shards, replicas)
    count, width = tokens.shape
    rows = w_query.shape[0]
    ff = w_gate.shape[1]
    wide_k = key_projection.shape[1]
    wide = width + 2 * wide_k
    x = tokens.T
    cot = cotangent.T
    cos, sin = tables(count)
    own_qkv = jnp.concatenate([w_query, key_projection, value_projection], axis=1)
    own_down = w_down.T
    gains = lax.all_gather(jnp.stack([attn_gain, mlp_gain]), "shard", axis=1, tiled=True).astype(F32)
    gain_one = gains[0][:, None]
    gain_two = gains[1][:, None]
    w_qkv = gather(grid, own_qkv, 0, 0)
    w_o = gather(grid, w_out, 0, 0)
    w_g = gather(grid, w_gate, 0, 0)
    w_u = gather(grid, w_up, 0, 0)
    w_d = gather(grid, own_down, 0, 1)

    normed, q, k, v = call(
        qkv_kernel, "qkv", [shape(width, count), shape(width, count), shape(wide_k, count), shape(wide_k, count)],
        2 * count * width * wide, in_specs=[whole()] * 5, out_specs=[whole()] * 4,
    )(x, gain_one, w_qkv, cos, sin)

    group = GROUP * HEAD_SIZE
    block_q = pl.BlockSpec((group, count), lambda i: (i, 0))
    block_k = pl.BlockSpec((HEAD_SIZE, count), lambda i: (i, 0))
    block_l = pl.BlockSpec((1, 8, count), lambda i: (i, 0, 0))
    block_t = pl.BlockSpec((HALF, count), lambda i: (0, 0))
    heads, lse = call(
        attend_kernel, "attend", [shape(width, count), shape(KEY_VALUE_HEADS, 8, count, dtype=F32)],
        2 * count * count * width, grid=(KEY_VALUE_HEADS,), in_specs=[block_q, block_k, block_k],
        out_specs=[block_q, block_l],
    )(q, k, v)

    middle, normed_two = call(
        middle_kernel, "middle", [shape(width, count, dtype=F32), shape(width, count)],
        2 * count * width * width, in_specs=[whole()] * 4, out_specs=[whole()] * 2,
    )(x, heads, w_o, gain_two)

    def fixed(*dims):
        return pl.BlockSpec(dims, lambda i: (0,) * len(dims))

    act = fixed(width, count)
    col = fixed(width, 1)
    square = fixed(width, width)
    block_w = pl.BlockSpec((width, BLOCK), lambda i: (0, i))
    g_down, g_gate, g_up, out, g_mid, g_heads, g_out = call(
        mlp_kernel, "mlp",
        [shape(width, ff), shape(width, ff), shape(width, ff), shape(width, count),
         shape(width, count, dtype=F32), shape(width, count), shape(width, width)],
        18 * count * width * ff, grid=(ff // BLOCK,),
        in_specs=[act, act, act, col, act, square, block_w, block_w, block_w],
        out_specs=[block_w, block_w, block_w, act, act, act, square],
        scratch=[pltpu.VMEM((width, count), F32), pltpu.VMEM((width, count), F32)],
    )(normed_two, cot, middle, gain_two, heads, w_o, w_g, w_u, w_d)

    g_q, g_k, g_v = call(
        attend_back_kernel, "attend_back", [shape(width, count), shape(wide_k, count), shape(wide_k, count)],
        5 * count * count * width, grid=(KEY_VALUE_HEADS,),
        in_specs=[block_q, block_k, block_k, block_q, block_l, block_q, block_t, block_t],
        out_specs=[block_q, block_k, block_k],
        scratch=[pltpu.VMEM((HEAD_SIZE, count), F32), pltpu.VMEM((HEAD_SIZE, count), F32)],
    )(q, k, v, heads, lse, g_heads, cos, sin)

    g_qkv = call(
        weight_kernel, "weights", shape(width, wide), 2 * count * width * wide,
        in_specs=[whole()] * 4, out_specs=whole(),
    )(normed, g_q, g_k, g_v)
    grad_tokens = call(
        tokens_kernel, "grad_tokens", shape(width, count), 2 * count * width * wide,
        in_specs=[whole()] * 7, out_specs=whole(),
    )(x, gain_one, w_qkv, g_q, g_k, g_v, g_mid)

    half_ff = ff // 2
    def by_rows(g):
        return g.reshape(2, rows, 2, g.shape[1] // 2).transpose(2, 0, 1, 3)

    t_gate = total(grid, by_rows(g_gate))
    t_up = total(grid, by_rows(g_up))
    t_down = total(grid, g_down.reshape(2, width // 2, 2, half_ff).transpose(0, 2, 1, 3))
    t_out = total(grid, by_rows(g_out))
    t_qkv = total(grid, by_rows(g_qkv))

    def rows_back(t):
        return t.transpose(1, 0, 2).reshape(rows, -1).astype(F32)

    t_gate, t_up, t_out, t_qkv = (rows_back(t) for t in (t_gate, t_up, t_out, t_qkv))
    t_down = t_down.reshape(width, half_ff).astype(F32)
    grad_attn_gain = jnp.sum(own_qkv.astype(F32) * t_qkv, axis=1) / attn_gain.astype(F32)
    grad_mlp_gain = jnp.sum(
        w_gate.astype(F32) * t_gate + w_up.astype(F32) * t_up, axis=1
    ) / mlp_gain.astype(F32)
    return (
        out.T,
        grad_tokens.T,
        grad_attn_gain,
        t_qkv[:, :width],
        t_qkv[:, width : width + wide_k],
        t_qkv[:, width + wide_k :],
        t_out,
        grad_mlp_gain,
        t_gate,
        t_up,
        t_down.T,
    )


def solution(mesh):
    tokens = P(AXES, None)
    split = P("shard", None)
    gain = P("shard")
    return jax.shard_map(
        functools.partial(local, mesh.shape["shard"], mesh.shape["replica"]),
        mesh=mesh,
        in_specs=(tokens, tokens, tokens, gain, split, split, split, split, gain, split, split, split),
        out_specs=(tokens, tokens, gain, split, split, split, split, gain, split, split, split),
        check_vma=False,
    )
```

```python
import functools
import math

import jax
import jax.numpy as jnp
import numpy as np
from jax import lax
from jax.experimental import pallas as pl
from jax.experimental.pallas import tpu as pltpu
from jax.sharding import PartitionSpec as P

QUERY_HEADS = 9
KEY_VALUE_HEADS = 3
HEAD_SIZE = 64
HALF = HEAD_SIZE // 2
GROUP = QUERY_HEADS // KEY_VALUE_HEADS
EPS = 1e-05
THETA = 100000.0
BF = jnp.bfloat16
F32 = jnp.float32
BLOCK = 256
VMEM_LIMIT = 32 * 2**20
AXES = ("shard", "replica")
LANES = 128
CORE, SIDE, SPLIT = 1, 2, 4


def nn(a, b):
    return lax.dot_general(a, b, (((1,), (0,)), ((), ())), preferred_element_type=F32)


def nt(a, b):
    return lax.dot_general(a, b, (((1,), (1,)), ((), ())), preferred_element_type=F32)


def tn(a, b):
    return lax.dot_general(a, b, (((0,), (0,)), ((), ())), preferred_element_type=F32)


def whole():
    return pl.BlockSpec(memory_space=pltpu.VMEM)


def call(kernel, name, outs, flops, grid=None, in_specs=None, out_specs=None, scratch=()):
    return pl.pallas_call(
        kernel,
        name=name,
        out_shape=outs,
        grid=grid or (),
        in_specs=in_specs,
        out_specs=out_specs,
        scratch_shapes=list(scratch),
        compiler_params=pltpu.CompilerParams(vmem_limit_bytes=VMEM_LIMIT),
        cost_estimate=pl.CostEstimate(flops=flops, bytes_accessed=8 * 2**20, transcendentals=0),
    )


def shape(*dims, dtype=BF):
    return jax.ShapeDtypeStruct(dims, dtype)


def tables(count):
    inverse = np.exp(np.arange(HALF, dtype=np.float32) * np.float32(-2.0 * math.log(THETA) / HEAD_SIZE))
    angles = jnp.arange(count, dtype=jnp.int32).astype(F32)[None, :] * jnp.asarray(inverse)[:, None]
    return jnp.cos(angles), jnp.sin(angles)

def smem():
    return pl.BlockSpec(memory_space=pltpu.SMEM)


def flip(a, b):
    return lax.rem(a + b, 2)


def pack_first_kernel(ids_ref, wq_ref, wk_ref, wv_ref, gain_one_ref, gain_two_ref, own_ref, half_ref):
    core = ids_ref[0]
    rows, wide = own_ref.shape
    size = rows // 2
    own_ref[...] = jnp.concatenate([wq_ref[...], wk_ref[...], wv_ref[...]], axis=1)
    half_ref[:size] = own_ref[pl.ds(core * size, size), :]
    gains = jnp.concatenate(
        [gain_one_ref[...].astype(F32), gain_two_ref[...].astype(F32), jnp.zeros((14, rows), F32)], axis=0
    )
    half_ref[size:] = jnp.concatenate([gains, jnp.zeros((16, wide - rows), F32)], axis=1).astype(BF)


def pack_rest_kernel(ids_ref, wo_ref, wg_ref, wu_ref, wd_ref, out_ref, *block_refs):
    core = ids_ref[0]
    rows, width = wo_ref.shape
    size = rows // 2
    mine = pl.ds(core * size, size)
    blocks = len(block_refs)
    out_ref[...] = wo_ref[mine, :]
    for b, ref in enumerate(block_refs):
        for s in range(2):
            cols = slice((s * blocks + b) * BLOCK, (s * blocks + b + 1) * BLOCK)
            ref[s * size : (s + 1) * size, :] = wg_ref[mine, cols]
            ref[(2 + s) * size : (3 + s) * size, :] = wu_ref[mine, cols]
        ref[4 * size : 6 * size, :] = wd_ref[pl.ds(core * rows, rows), b * BLOCK : (b + 1) * BLOCK]


def fill(to, core, shard, own, first, second, size):
    rows = 2 * size
    to[pl.ds(shard * rows, rows), :] = own
    to[pl.ds((1 - shard) * rows + core * size, size), :] = first
    to[pl.ds((1 - shard) * rows + (1 - core) * size, size), :] = second


def qkv_kernel(ids_ref, x_ref, own_ref, half_ref, first_ref, second_ref, cos_ref, sin_ref,
               n_ref, q_ref, k_ref, v_ref, w_ref, gains_ref):
    core, shard = ids_ref[0], ids_ref[1]
    rows = own_ref.shape[0]
    size = rows // 2
    fill(w_ref, core, shard, own_ref[...], first_ref[:size], second_ref[:size], size)
    padded = -(-rows // LANES) * LANES
    for ref, side in ((half_ref, shard), (first_ref, 1 - shard)):
        gains_ref[pl.ds(side * rows, rows), :] = ref[size:, :padded].astype(F32).T[:rows]
    count = x_ref.shape[1]
    gain = gains_ref[:, 0:1]
    width_q = q_ref.shape[0]
    width_k = k_ref.shape[0]
    for at in range(0, count, BLOCK):
        cols = slice(at, at + BLOCK)
        x = x_ref[:, cols].astype(F32)
        r = lax.rsqrt(jnp.mean(x * x, axis=0, keepdims=True) + EPS)
        n = (x * r * gain).astype(BF)
        n_ref[:, cols] = n
        y = tn(w_ref[...], n)
        c = cos_ref[:, cols]
        s = sin_ref[:, cols]
        cq, sq = c * 0.125, s * 0.125
        for head in range((width_q + width_k) // HEAD_SIZE):
            row = head * HEAD_SIZE
            u1 = y[row : row + HALF]
            u2 = y[row + HALF : row + HEAD_SIZE]
            if row < width_q:
                q_ref[row : row + HALF, cols] = (u1 * cq - u2 * sq).astype(BF)
                q_ref[row + HALF : row + HEAD_SIZE, cols] = (u2 * cq + u1 * sq).astype(BF)
            else:
                row -= width_q
                k_ref[row : row + HALF, cols] = (u1 * c - u2 * s).astype(BF)
                k_ref[row + HALF : row + HEAD_SIZE, cols] = (u2 * c + u1 * s).astype(BF)
        v_ref[:, cols] = y[width_q + width_k :].astype(BF)


def causal(s):
    low = s.shape[0] - BLOCK
    rows = lax.broadcasted_iota(jnp.int32, (BLOCK, BLOCK), 0)
    cols = lax.broadcasted_iota(jnp.int32, (BLOCK, BLOCK), 1)
    keep = jnp.concatenate([rows <= cols] * (s.shape[1] // BLOCK), axis=1)
    last = jnp.where(keep, s[low:], -1e30)
    return last if low == 0 else jnp.concatenate([s[:low], last], axis=0)


def beside(ref, cols):
    return jnp.concatenate(
        [ref[h * HEAD_SIZE : (h + 1) * HEAD_SIZE, cols] for h in range(GROUP)], axis=1
    )


def attend_kernel(q_ref, k_ref, v_ref, o_ref, lse_ref):
    count = q_ref.shape[1]
    keys = k_ref[...].astype(F32).T.astype(BF)
    for at in range(0, count, BLOCK):
        end = at + BLOCK
        cols = slice(at, end)
        s = causal(nn(keys[:end], beside(q_ref, cols)))
        top = jnp.max(s, axis=0, keepdims=True)
        p = jnp.exp(s - top)
        total = jnp.sum(p, axis=0, keepdims=True)
        o = nn(v_ref[:, :end], p.astype(BF)) / total
        lse = top + jnp.log(total)
        for h in range(GROUP):
            part = slice(h * BLOCK, (h + 1) * BLOCK)
            o_ref[h * HEAD_SIZE : (h + 1) * HEAD_SIZE, cols] = o[:, part].astype(BF)
            lse_ref[0, h : h + 1, cols] = lse[:, part]


def middle_kernel(ids_ref, x_ref, heads_ref, own_ref, first_ref, second_ref, gain_ref, mid_ref, n_ref, w_ref):
    fill(w_ref, ids_ref[0], ids_ref[1], own_ref[...], first_ref[...], second_ref[...], first_ref.shape[0])
    count = x_ref.shape[1]
    gain = gain_ref[:, 1:2]
    for at in range(0, count, BLOCK):
        cols = slice(at, at + BLOCK)
        m = x_ref[:, cols].astype(F32) + tn(w_ref[...], heads_ref[:, cols])
        r = lax.rsqrt(jnp.mean(m * m, axis=0, keepdims=True) + EPS)
        mid_ref[:, cols] = m
        n_ref[:, cols] = (m * r * gain).astype(BF)


def norm_back(x, gain, grad):
    r = lax.rsqrt(jnp.mean(x * x, axis=0, keepdims=True) + EPS)
    scaled = gain * grad
    dot = jnp.mean(scaled * x, axis=0, keepdims=True)
    return r * scaled - x * (r * r * r * dot)


def put(refs, ids_ref, half, shard, lane_half, rows, value):
    core = ids_ref[0]
    keep_ref, send_ref = refs
    s, y = flip(ids_ref[1], shard), flip(ids_ref[2], lane_half)
    one, two = jnp.where(core == 0, s, y), jnp.where(core == 0, y, s)

    @pl.when(core == half)
    def _():
        keep_ref[one, two, rows] = value

    @pl.when(core != half)
    def _():
        send_ref[two, one, rows] = value


def mlp_block(ids_ref, n_ref, cot_ref, g0_ref, g1_ref, u0_ref, u1_ref, d_ref, first_ref, second_ref,
              acc_in, gn_in, refs, acc_ref, gn_ref, w, wd, act):
    core, shard = ids_ref[0], ids_ref[1]
    rows = g0_ref.shape[0]
    size = rows // 2
    hid = 2 * BLOCK
    for i, ref in enumerate((g0_ref, g1_ref, u0_ref, u1_ref)):
        part = slice(i * size, (i + 1) * size)
        fill(w.at[:, i * BLOCK : (i + 1) * BLOCK], core, shard, ref[...], first_ref[part], second_ref[part], size)
    for s in range(2):
        cols = slice(s * BLOCK, (s + 1) * BLOCK)

        @pl.when(shard == s)
        def _():
            wd[:, cols] = d_ref[...]

        @pl.when(shard != s)
        def _():
            wd[pl.ds(core * rows, rows), cols] = first_ref[4 * size : 6 * size]
            wd[pl.ds((1 - core) * rows, rows), cols] = second_ref[4 * size : 6 * size]

    count = n_ref.shape[1]
    for at in range(0, count, BLOCK):
        cols = slice(at, at + BLOCK)
        both = tn(w[...], n_ref[:, cols])
        gate, up = both[:hid], both[hid:]
        gh = tn(wd[...], cot_ref[:, cols])
        sig = 0.5 * jnp.tanh(0.5 * gate) + 0.5
        a = gate * sig
        act[:hid, cols] = (a * up).astype(BF)
        act[hid : 2 * hid, cols] = (gh * up * (sig + a * (1.0 - sig))).astype(BF)
        act[2 * hid :, cols] = (gh * a).astype(BF)
        part = nn(wd[...], act[:hid, cols])
        gpart = nn(w[...], act[hid:, cols])
        acc_ref[:, cols] = part if acc_in is None else acc_in[:, cols] + part
        gn_ref[:, cols] = gpart if gn_in is None else gn_in[:, cols] + gpart
    for s in range(2):
        gd = nt(cot_ref[...], act[s * BLOCK : (s + 1) * BLOCK]).astype(BF)
        gg = nt(n_ref[...], act[hid + s * BLOCK : hid + (s + 1) * BLOCK]).astype(BF)
        gu = nt(n_ref[...], act[2 * hid + s * BLOCK : 2 * hid + (s + 1) * BLOCK]).astype(BF)
        for z in range(2):
            lanes = slice(z * LANES, (z + 1) * LANES)
            for half in range(2):
                part = slice(half * rows, (half + 1) * rows)
                put(refs, ids_ref, half, s, z, slice(0, rows), gd[part, lanes])
                put(refs, ids_ref, s, half, z, slice(rows, 2 * rows), gg[part, lanes])
                put(refs, ids_ref, s, half, z, slice(2 * rows, 3 * rows), gu[part, lanes])


def mlp_one_kernel(ids_ref, n_ref, cot_ref, g0, g1, u0, u1, d, first, second, keep, send, acc, gn, *scratch):
    mlp_block(ids_ref, n_ref, cot_ref, g0, g1, u0, u1, d, first, second, None, None, (keep, send), acc, gn, *scratch)


def mlp_two_kernel(ids_ref, n_ref, cot_ref, g0, g1, u0, u1, d, first, second, acc_in, gn_in,
                   keep, send, acc, gn, *scratch):
    mlp_block(ids_ref, n_ref, cot_ref, g0, g1, u0, u1, d, first, second, acc_in, gn_in, (keep, send), acc, gn, *scratch)


def mlp_three_kernel(ids_ref, n_ref, cot_ref, g0, g1, u0, u1, d, first, second, acc_in, gn_in,
                     mid_ref, gain_ref, heads_ref, wo_ref,
                     keep, send, out_ref, gmid_ref, gheads_ref, acc, gn, *scratch):
    mlp_block(ids_ref, n_ref, cot_ref, g0, g1, u0, u1, d, first, second, acc_in, gn_in, (keep, send), acc, gn, *scratch)
    width, count = n_ref.shape
    gain = gain_ref[:, 1:2]
    low = []
    for at in range(0, count, BLOCK):
        cols = slice(at, at + BLOCK)
        mid = mid_ref[:, cols]
        out_ref[:, cols] = (mid + acc[:, cols]).astype(BF)
        gm = cot_ref[:, cols].astype(F32) + norm_back(mid, gain, gn[:, cols])
        gmid_ref[:, cols] = gm
        low.append(gm.astype(BF))
        gheads_ref[:, cols] = nn(wo_ref[...], low[-1]).astype(BF)
    g = nt(heads_ref[...], jnp.concatenate(low, axis=1)).astype(BF)
    per = -(-(-(-width // LANES)) // 2)
    size = width // 4
    base = 3 * width // 2
    rest = keep.shape[2] - base - per * size
    for s in range(2):
        for half in range(2):
            rows = slice((2 * s + half) * size, (2 * s + half + 1) * size)
            for i in range(2 * per):
                end = min((i + 1) * LANES, width)
                value = g[rows, i * LANES : end] if end > i * LANES else None
                if value is None:
                    value = jnp.zeros((size, LANES), BF)
                elif end < (i + 1) * LANES:
                    value = jnp.concatenate([value, jnp.zeros((size, (i + 1) * LANES - end), BF)], axis=1)
                at = base + (i % per) * size
                put((keep, send), ids_ref, half, s, i // per, slice(at, at + size), value)
            if rest:
                for y in range(2):
                    put((keep, send), ids_ref, half, s, y, slice(base + per * size, base + per * size + rest),
                        jnp.zeros((rest, LANES), BF))


def attend_back_kernel(q_ref, k_ref, v_ref, o_ref, lse_ref, go_ref, cos_ref, sin_ref,
                       gq_ref, gk_ref, gv_ref, dk_ref, dv_ref):
    count = q_ref.shape[1]
    keys = k_ref[...].astype(F32).T.astype(BF)
    values = v_ref[...].astype(F32).T.astype(BF)
    dk_ref[...] = jnp.zeros_like(dk_ref)
    dv_ref[...] = jnp.zeros_like(dv_ref)
    for at in range(0, count, BLOCK):
        end = at + BLOCK
        cols = slice(at, end)
        q = beside(q_ref, cols)
        go = beside(go_ref, cols)
        delta = jnp.sum(go.astype(F32) * beside(o_ref, cols).astype(F32), axis=0, keepdims=True)
        lse = jnp.concatenate([lse_ref[0, h : h + 1, cols] for h in range(GROUP)], axis=1)
        s = causal(nn(keys[:end], q))
        p = jnp.exp(s - lse)
        ds = (p * (nn(values[:end], go) - delta)).astype(BF)
        dv_ref[:, :end] += nt(go, p.astype(BF))
        dk_ref[:, :end] += nt(q, ds)
        dq = nn(k_ref[:, :end], ds)
        c = cos_ref[:, cols] * 0.125
        sn = sin_ref[:, cols] * 0.125
        for h in range(GROUP):
            part = slice(h * BLOCK, (h + 1) * BLOCK)
            g1, g2 = dq[:HALF, part], dq[HALF:, part]
            row = h * HEAD_SIZE
            gq_ref[row : row + HALF, cols] = (g1 * c + g2 * sn).astype(BF)
            gq_ref[row + HALF : row + HEAD_SIZE, cols] = (g2 * c - g1 * sn).astype(BF)
    c = cos_ref[...]
    sn = sin_ref[...]
    g1, g2 = dk_ref[:HALF], dk_ref[HALF:]
    gk_ref[:HALF] = (g1 * c + g2 * sn).astype(BF)
    gk_ref[HALF:] = (g2 * c - g1 * sn).astype(BF)
    gv_ref[...] = dv_ref[...].astype(BF)


def weight_kernel(ids_ref, n_ref, *refs):
    count = (len(refs) - 2) // 3
    keep_ref, send_ref = refs[-2:]
    size, lanes = keep_ref.shape[2:]
    g = jnp.concatenate([refs[i * count + j][...] for i in range(3) for j in range(count)], axis=0)
    wide = g.shape[0]
    for z in range(2):
        end = min((z + 1) * lanes, wide)
        w = nt(n_ref[...], g[z * lanes : end]).astype(BF)
        if end < (z + 1) * lanes:
            w = jnp.concatenate([w, jnp.zeros((w.shape[0], (z + 1) * lanes - end), BF)], axis=1)
        for s in range(2):
            for half in range(2):
                at = (2 * s + half) * size
                put((keep_ref, send_ref), ids_ref, half, s, z, slice(0, size), w[at : at + size])


def tokens_kernel(x_ref, gain_ref, w_ref, gmid_ref, *refs):
    out_ref = refs[-1]
    parts = (len(refs) - 1) // 3
    count = x_ref.shape[1]
    gain = gain_ref[:, 0:1]
    for at in range(0, count, BLOCK):
        cols = slice(at, at + BLOCK)
        g = jnp.concatenate([refs[i * parts + j][:, cols] for i in range(3) for j in range(parts)], axis=0)
        gn = nn(w_ref[...], g)
        x = x_ref[:, cols].astype(F32)
        out_ref[:, cols] = (gmid_ref[:, cols] + norm_back(x, gain, gn)).astype(BF)


def plus(a, b):
    return (a.astype(F32) + b.astype(F32)).astype(BF)


def add_first_kernel(*refs):
    count = (len(refs) - 2) // 2
    send_ref, keep_ref = refs[-2:]
    at = 0
    for i in range(count):
        a, b = refs[i], refs[count + i]
        rows = slice(at, at + a.shape[2])
        at += a.shape[2]
        for j in range(2):
            send_ref[j, rows] = plus(a[1, j], b[1, j])
            keep_ref[j, rows] = plus(a[0, j], b[0, j])


def add_second_kernel(a_ref, b_ref, send_ref, keep_ref):
    send_ref[...] = plus(a_ref[1], b_ref[1])
    keep_ref[...] = plus(a_ref[0], b_ref[0])


def add_split_kernel(ids_ref, a_ref, b_ref, send_ref, keep_ref):
    z = ids_ref[3]
    rows = send_ref.shape[0]
    for ref, side in ((send_ref, 1 - z), (keep_ref, z)):
        part = pl.ds(side * rows, rows)
        ref[...] = plus(a_ref[part, :], b_ref[part, :])


def add_kernel(a_ref, b_ref, out_ref):
    out_ref[...] = plus(a_ref[...], b_ref[...])


def join_kernel(ids_ref, a_ref, b_ref, out_ref):
    z = ids_ref[3]
    rows = a_ref.shape[0]
    out_ref[pl.ds(z * rows, rows), :] = a_ref[...]
    out_ref[pl.ds((1 - z) * rows, rows), :] = b_ref[...]


def chosen(ids_ref, refs, half, y, rows):
    core, side = ids_ref[0], ids_ref[2]
    own, own_other, far, far_other = (ref[rows] for ref in refs)
    near = jnp.where(side == y, own, own_other)
    return jnp.where(core == half, near, jnp.where(side == y, far, far_other)).astype(F32)


def as_row(column_sums):
    rows = column_sums.shape[0]
    padded = -(-rows // LANES) * LANES
    if padded > rows:
        column_sums = jnp.concatenate([column_sums, jnp.zeros((padded - rows, LANES), F32)], axis=0)
    return jnp.sum(column_sums.T, axis=0, keepdims=True)[:, :rows]


def finish_mlp_kernel(ids_ref, a0, a1, a2, a3, b0, b1, b2, b3, wg_ref, wu_ref, gain_ref,
                      gate_ref, up_ref, down_ref, out_ref, gain_out_ref):
    rows, ff = gate_ref.shape
    blocks = ff // 2 // BLOCK
    total = jnp.zeros((rows, LANES), F32)
    for b in range(blocks):
        refs = (a0, a1, a2, a3) if b == 0 else (b0, b1, b2, b3)
        base = 3 * max(b - 1, 0) * rows
        for z in range(2):
            for half in range(2):
                at = b * BLOCK + z * LANES
                down_ref[half * rows : (half + 1) * rows, at : at + LANES] = chosen(
                    ids_ref, refs, half, z, slice(base, base + rows))
                at += half * blocks * BLOCK
                for i, w_ref, to in ((1, wg_ref, gate_ref), (2, wu_ref, up_ref)):
                    g = chosen(ids_ref, refs, half, z, slice(base + i * rows, base + (i + 1) * rows))
                    to[:, at : at + LANES] = g
                    total += g * w_ref[:, at : at + LANES].astype(F32)
    gain_out_ref[...] = as_row(total) / gain_ref[...].astype(F32)
    width = out_ref.shape[1]
    pieces = -(-width // LANES)
    per = -(-pieces // 2)
    size = rows // 2
    base = 3 * (blocks - 1) * rows
    for half in range(2):
        for i in range(pieces):
            end = min((i + 1) * LANES, width)
            at = base + (i % per) * size
            g = chosen(ids_ref, (b0, b1, b2, b3), half, i // per, slice(at, at + size))
            out_ref[half * size : (half + 1) * size, i * LANES : end] = g[:, : end - i * LANES]


def finish_qkv_kernel(ids_ref, a0, a1, a2, a3, w_ref, gain_ref, q_ref, k_ref, v_ref, gain_out_ref, sum_ref):
    size, lanes = a0.shape
    wide_q, wide_k = q_ref.shape[1], k_ref.shape[1]
    wide = w_ref.shape[1]
    for half in range(2):
        rows = slice(half * size, (half + 1) * size)
        parts = [chosen(ids_ref, (a0, a1, a2, a3), half, z, slice(0, size)) for z in range(2)]
        g = jnp.concatenate(parts, axis=1)[:, :wide]
        q_ref[rows] = g[:, :wide_q]
        k_ref[rows] = g[:, wide_q : wide_q + wide_k]
        v_ref[rows] = g[:, wide_q + wide_k :]
        sums = jnp.sum(g * w_ref[rows].astype(F32), axis=1, keepdims=True)
        sum_ref[rows] = sums * (lax.broadcasted_iota(jnp.int32, (size, LANES), 1) == 0).astype(F32)
    gain_out_ref[...] = as_row(sum_ref[...]) / gain_ref[...].astype(F32)


class Grid:
    def __init__(self, shards, replicas):
        self.shards, self.replicas = shards, replicas
        self.shard = lax.axis_index("shard")
        self.replica = lax.axis_index("replica")
        self.rest = [1 << i for i in range(3, replicas.bit_length() - 1)]
        self.ids = jnp.stack(
            [self.side(CORE), self.shard, self.side(SIDE), self.side(SPLIT)]
        ).astype(jnp.int32)

    def side(self, bit):
        return (self.replica // bit) % 2

    def swap(self, a, even, odd=None):
        odd = even if odd is None else odd
        pairs = []
        for s in range(self.shards):
            for r in range(self.replicas):
                shard, bit = odd if r % 2 else even
                pairs.append((s * self.replicas + r, (s ^ shard) * self.replicas + (r ^ bit)))
        return lax.ppermute(a, AXES, pairs)


def tie(values, others):
    return lax.optimization_barrier((tuple(values), tuple(others)))[0]


def flow(grid, keeps, sends, split):
    rows = sum(k.shape[2] for k in keeps)
    lanes = keeps[0].shape[3]
    ops = 2 * 10**9
    gots = [grid.swap(s, (0, CORE)) for s in sends]
    after = yield sends
    gots = tie(gots, after)
    two = shape(2, rows, lanes)
    send, keep = call(add_first_kernel, "add_core", [two, two], ops,
                      in_specs=[whole()] * (2 * len(keeps)), out_specs=[whole()] * 2)(*keeps, *gots)
    got = grid.swap(send, (1, 0), (0, SIDE))
    after = yield [send]
    (got,) = tie([got], after)
    one = shape(rows, lanes)
    send, keep = call(add_second_kernel, "add_second", [one, one], ops,
                      in_specs=[whole()] * 2, out_specs=[whole()] * 2)(keep, got)
    got = grid.swap(send, (0, SIDE), (1, 0))
    after = yield [send]
    (got,) = tie([got], after)

    def add(a, b):
        return call(add_kernel, "add", shape(*a.shape), ops, in_specs=[whole()] * 2, out_specs=whole())(a, b)

    if split:
        half = shape(rows // 2, lanes)
        send, keep = call(add_split_kernel, "add_split", [half, half], ops,
                          in_specs=[smem()] + [whole()] * 2, out_specs=[whole()] * 2)(grid.ids, keep, got)
    else:
        send = keep = add(keep, got)
    got = grid.swap(send, (0, SPLIT))
    after = yield [send]
    (got,) = tie([got], after)
    a = add(keep, got)
    for bit in grid.rest:
        got = grid.swap(a, (0, bit))
        after = yield [a]
        (got,) = tie([got], after)
        a = add(a, got)
    if split:
        got = grid.swap(a, (0, SPLIT))
        after = yield [a]
        (got,) = tie([got], after)
        a = call(join_kernel, "join", one, ops, in_specs=[smem()] + [whole()] * 2, out_specs=whole())(grid.ids, a, got)
    b = grid.swap(a, (0, SIDE))
    far = grid.swap(a, (0, CORE))
    after = yield [a]
    (b,) = tie([b], after)
    far_b = grid.swap(b, (0, CORE))
    yield a, b, far, far_b


def local(shards, replicas, tokens, cotangent, lengths, attn_gain, w_query, key_projection,
          value_projection, w_out, mlp_gain, w_gate, w_up, w_down):
    grid = Grid(shards, replicas)
    ids = grid.ids
    count, width = tokens.shape
    rows = w_query.shape[0]
    size = rows // 2
    ff = w_gate.shape[1]
    blocks = ff // 2 // BLOCK
    wide_k = key_projection.shape[1]
    wide = width + 2 * wide_k
    x = tokens.T
    cot = cotangent.T
    cos, sin = tables(count)
    own_down = w_down.T
    gain_row_one, gain_row_two = attn_gain[None], mlp_gain[None]

    own_qkv, half_qkv = call(
        pack_first_kernel, "pack_first", [shape(rows, wide), shape(size + 16, wide)], 10**6,
        in_specs=[smem()] + [whole()] * 5, out_specs=[whole()] * 2,
    )(ids, w_query, key_projection, value_projection, gain_row_one, gain_row_two)
    first_qkv = grid.swap(half_qkv, (1, 0))
    (w_out_,) = tie([w_out], [half_qkv])
    half_out, *halves = call(
        pack_rest_kernel, "pack_rest", [shape(size, width)] + [shape(6 * size, BLOCK)] * blocks, 10**6,
        in_specs=[smem()] + [whole()] * 4, out_specs=[whole()] * (1 + blocks),
    )(ids, w_out_, w_gate, w_up, own_down)
    first_out = grid.swap(half_out, (1, 0))
    firsts = [grid.swap(h, (1, 0)) for h in halves]
    (first_qkv,) = tie([first_qkv], [half_out])
    second_qkv = grid.swap(first_qkv, (0, CORE))

    normed, q, k, v, w_qkv, gains = call(
        qkv_kernel, "qkv",
        [shape(width, count), shape(width, count), shape(wide_k, count), shape(wide_k, count), shape(width, wide),
         shape(width, 16, dtype=F32)],
        2 * count * width * wide, in_specs=[smem()] + [whole()] * 7, out_specs=[whole()] * 6,
    )(ids, x, own_qkv, half_qkv, first_qkv, second_qkv, cos, sin)

    (first_out,) = tie([first_out], [q])
    second_out = grid.swap(first_out, (0, CORE))
    group = GROUP * HEAD_SIZE
    heads, lse = call(
        attend_kernel, "attend", [shape(width, count), shape(KEY_VALUE_HEADS, 8, count, dtype=F32)],
        8 * count * count * width, grid=(KEY_VALUE_HEADS,),
        in_specs=[pl.BlockSpec((group, count), lambda i: (i, 0))] + [pl.BlockSpec((HEAD_SIZE, count), lambda i: (i, 0))] * 2,
        out_specs=[pl.BlockSpec((group, count), lambda i: (i, 0)), pl.BlockSpec((1, 8, count), lambda i: (i, 0, 0))],
    )(q, k, v)
    (first_a,) = tie(firsts[:1], [heads])
    second_a = grid.swap(first_a, (0, CORE))

    middle, normed_two, w_o = call(
        middle_kernel, "middle", [shape(width, count, dtype=F32), shape(width, count), shape(width, width)],
        2 * count * width * width, in_specs=[smem()] + [whole()] * 6, out_specs=[whole()] * 3,
    )(ids, x, heads, w_out, first_out, second_out, gains)

    def fixed(*dims):
        return pl.BlockSpec(dims, lambda i: (0,) * len(dims))

    act = fixed(width, count)
    scratch = [pltpu.VMEM((width, 4 * BLOCK), BF), pltpu.VMEM((width, 2 * BLOCK), BF), pltpu.VMEM((6 * BLOCK, count), BF)]
    float_act = shape(width, count, dtype=F32)

    def of_block(b):
        near = pl.BlockSpec((rows, BLOCK), lambda i: (0, b))
        far = pl.BlockSpec((rows, BLOCK), lambda i: (0, blocks + b))
        down = pl.BlockSpec((width, BLOCK), lambda i: (0, b))
        pack = fixed(6 * size, BLOCK)
        return [smem(), act, act, near, far, near, far, down, pack, pack]

    def mlp(kernel, b, outs, out_specs, first, second, more, more_specs, extra=()):
        return call(
            kernel, "mlp", outs, 18 * count * width * ff // blocks, grid=(1,), in_specs=of_block(b) + more_specs,
            out_specs=out_specs, scratch=list(extra) + scratch,
        )(ids, normed_two, cot, w_gate, w_gate, w_up, w_up, own_down, first, second, *more)

    part = (2, 2, 3 * rows, LANES)
    keep_a, send_a, acc, gn = mlp(
        mlp_one_kernel, 0, [shape(*part)] * 2 + [float_act] * 2, [fixed(*part)] * 2 + [act] * 2, first_a, second_a, [], [])
    flow_a = flow(grid, [keep_a], [send_a], True)
    sent = next(flow_a)
    (first_b,) = tie(firsts[1:2], [acc])
    second_b = grid.swap(first_b, (0, CORE))
    normed_two, first_b = tie([normed_two, first_b], sent)
    keep_b, send_b, acc, gn = mlp(
        mlp_two_kernel, 1, [shape(*part)] * 2 + [float_act] * 2, [fixed(*part)] * 2 + [act] * 2, first_b, second_b,
        [acc, gn], [act] * 2)
    sent = flow_a.send([acc])
    (first_c,) = tie(firsts[2:3], [acc])
    second_c = grid.swap(first_c, (0, CORE))
    normed_two, first_c = tie([normed_two, first_c], sent)
    per = -(-(-(-width // LANES)) // 2)
    rows_c = -(-(3 * rows + per * size) // 32) * 32
    part_c = (2, 2, rows_c, LANES)
    keep_c, send_c, out, g_mid, g_heads = mlp(
        mlp_three_kernel, 2, [shape(*part_c)] * 2 + [shape(width, count), float_act, shape(width, count)],
        [fixed(*part_c)] * 2 + [act] * 3, first_c, second_c,
        [acc, gn, middle, gains, heads, w_o], [act, act, act, fixed(width, 16), act, fixed(width, width)],
        extra=[pltpu.VMEM((width, count), F32)] * 2)
    flow_b = flow(grid, [keep_b, keep_c], [send_b, send_c], True)
    sent = list(next(flow_b))
    sent += flow_a.send([g_heads])

    g_q, g_k, g_v = [], [], []
    for i in range(KEY_VALUE_HEADS):
        (g_heads_,) = tie([g_heads], sent)
        block_q = pl.BlockSpec((group, count), lambda j, i=i: (i, 0))
        block_k = pl.BlockSpec((HEAD_SIZE, count), lambda j, i=i: (i, 0))
        block_l = pl.BlockSpec((1, 8, count), lambda j, i=i: (i, 0, 0))
        out_q, out_k = fixed(group, count), fixed(HEAD_SIZE, count)
        a, b, c = call(
            attend_back_kernel, "attend_back", [shape(group, count), shape(HEAD_SIZE, count), shape(HEAD_SIZE, count)],
            4 * count * count * width, grid=(1,),
            in_specs=[block_q, block_k, block_k, block_q, block_l, block_q, fixed(HALF, count), fixed(HALF, count)],
            out_specs=[out_q, out_k, out_k],
            scratch=[pltpu.VMEM((HEAD_SIZE, count), F32)] * 2,
        )(q, k, v, heads, lse, g_heads_, cos, sin)
        g_q.append(a)
        g_k.append(b)
        g_v.append(c)
        sent = []
        if i == 0:
            sent += flow_b.send([c])
        sent += flow_a.send([c])
    grads = g_q + g_k + g_v

    lanes = -(-wide // (2 * LANES)) * LANES
    part_three = (2, 2, size, lanes)
    normed_, *_ = tie([normed], sent)
    keep_d, send_d = call(
        weight_kernel, "weights", [shape(*part_three), shape(*part_three)], 2 * count * width * wide,
        in_specs=[smem()] + [whole()] * 10, out_specs=[whole()] * 2,
    )(ids, normed_, *grads)
    flow_d = flow(grid, [keep_d], [send_d], False)
    sent = next(flow_d)
    x_, *_ = tie([x], sent)
    grad_tokens = call(
        tokens_kernel, "grad_tokens", shape(width, count), 2 * count * width * wide,
        in_specs=[whole()] * 13, out_specs=whole(),
    )(x_, gains, w_qkv, g_mid, *grads)

    sums = {}
    flows = {"a": flow_a, "b": flow_b, "d": flow_d}
    last = [grad_tokens]
    while flows:
        for name in list(flows):
            sent = flows[name].send(last)
            if len(sent) == 4:
                sums[name] = sent
                del flows[name]

    g_gate, g_up, g_down, g_out, g_gain_two = call(
        finish_mlp_kernel, "finish_mlp",
        [shape(rows, ff, dtype=F32), shape(rows, ff, dtype=F32), shape(width, ff // 2, dtype=F32),
         shape(rows, width, dtype=F32), shape(1, rows, dtype=F32)],
        10**7, in_specs=[smem()] + [whole()] * 11, out_specs=[whole()] * 5,
    )(ids, *sums["a"], *sums["b"], w_gate, w_up, gain_row_two)
    g_query, g_key, g_value, g_gain_one = call(
        finish_qkv_kernel, "finish_qkv",
        [shape(rows, width, dtype=F32), shape(rows, wide_k, dtype=F32), shape(rows, wide_k, dtype=F32),
         shape(1, rows, dtype=F32)],
        10**7, in_specs=[smem()] + [whole()] * 6, out_specs=[whole()] * 4, scratch=[pltpu.VMEM((rows, LANES), F32)],
    )(ids, *sums["d"], own_qkv, gain_row_one)
    return (
        out.T,
        grad_tokens.T,
        g_gain_one[0],
        g_query,
        g_key,
        g_value,
        g_out,
        g_gain_two[0],
        g_gate,
        g_up,
        g_down.T,
    )


def solution(mesh):
    tokens = P(AXES, None)
    split = P("shard", None)
    gain = P("shard")
    return jax.shard_map(
        functools.partial(local, mesh.shape["shard"], mesh.shape["replica"]),
        mesh=mesh,
        in_specs=(tokens, tokens, tokens, gain, split, split, split, split, gain, split, split, split),
        out_specs=(tokens, tokens, gain, split, split, split, split, gain, split, split, split),
        check_vma=False,
    )
```

```python
import functools
import math

import jax
import jax.numpy as jnp
import numpy as np
from jax import lax
from jax.experimental import pallas as pl
from jax.experimental.pallas import tpu as pltpu
from jax.sharding import PartitionSpec as P

QUERY_HEADS = 9
KEY_VALUE_HEADS = 3
HEAD_SIZE = 64
HALF = HEAD_SIZE // 2
GROUP = QUERY_HEADS // KEY_VALUE_HEADS
EPS = 1e-05
THETA = 100000.0
BF = jnp.bfloat16
F32 = jnp.float32
BLOCK = 256
AXES = ("shard", "replica")
LANES = 128
CORE, SIDE, SPLIT = 1, 2, 4


def nn(a, b):
    return lax.dot_general(a, b, (((1,), (0,)), ((), ())), preferred_element_type=F32)


def nt(a, b):
    return lax.dot_general(a, b, (((1,), (1,)), ((), ())), preferred_element_type=F32)


def tn(a, b):
    return lax.dot_general(a, b, (((0,), (0,)), ((), ())), preferred_element_type=F32)


def whole():
    return pl.BlockSpec(memory_space=pltpu.VMEM)


def call(kernel, name, outs, flops, grid=None, in_specs=None, out_specs=None, scratch=(), limit=16, weight=1, aliases=None):
    return pl.pallas_call(
        kernel,
        name=name,
        out_shape=outs,
        grid=grid or (),
        in_specs=in_specs,
        out_specs=out_specs,
        scratch_shapes=list(scratch),
        compiler_params=pltpu.CompilerParams(vmem_limit_bytes=limit * 2**20),
        input_output_aliases=aliases or {},
        cost_estimate=pl.CostEstimate(flops=weight * flops, bytes_accessed=min(8 * 2**20, weight * flops), transcendentals=0),
    )


def copied(*dims):
    return pl.BlockSpec(dims, lambda i: (0,) * len(dims))


def shape(*dims, dtype=BF):
    return jax.ShapeDtypeStruct(dims, dtype)


def tables(count):
    inverse = np.exp(np.arange(HALF, dtype=np.float32) * np.float32(-2.0 * math.log(THETA) / HEAD_SIZE))
    angles = jnp.arange(count, dtype=jnp.int32).astype(F32)[None, :] * jnp.asarray(inverse)[:, None]
    return jnp.cos(angles), jnp.sin(angles)

def smem():
    return pl.BlockSpec(memory_space=pltpu.SMEM)


def flip(a, b):
    return lax.rem(a + b, 2)


def pack_first_kernel(ids_ref, wq_ref, wk_ref, wv_ref, own_ref, half_ref):
    size = half_ref.shape[0]
    own_ref[...] = jnp.concatenate([wq_ref[...], wk_ref[...], wv_ref[...]], axis=1)
    half_ref[...] = own_ref[pl.ds(ids_ref[0] * size, size), :]


def pack_kernel(ids_ref, wg_ref, wu_ref, wd_ref, wo_ref, *out_refs):
    core = ids_ref[0]
    rows, width = wo_ref.shape
    size = rows // 2
    mine = pl.ds(core * size, size)
    blocks = len(out_refs)
    for b, out_ref in enumerate(out_refs):
        for s in range(2):
            cols = slice((s * blocks + b) * BLOCK, (s * blocks + b + 1) * BLOCK)
            out_ref[s * size : (s + 1) * size, :] = wg_ref[mine, cols]
            out_ref[(2 + s) * size : (3 + s) * size, :] = wu_ref[mine, cols]
        out_ref[4 * size : 6 * size, :] = wd_ref[pl.ds(core * rows, rows), b * BLOCK : (b + 1) * BLOCK]
    for i in range(-(-width // BLOCK)):
        end = min((i + 1) * BLOCK, width)
        piece = wo_ref[mine, i * BLOCK : end]
        if end < (i + 1) * BLOCK:
            piece = jnp.concatenate([piece, jnp.zeros((size, (i + 1) * BLOCK - end), BF)], axis=1)
        out_refs[0][(6 + i) * size : (7 + i) * size, :] = piece


def fill(to, core, shard, own, first, second, size):
    rows = 2 * size
    to[pl.ds(shard * rows, rows), :] = own
    to[pl.ds((1 - shard) * rows + core * size, size), :] = first
    to[pl.ds((1 - shard) * rows + (1 - core) * size, size), :] = second


def qkv_kernel(ids_ref, x_ref, gain_ref, own_ref, first_ref, second_ref, cos_ref, sin_ref,
               n_ref, q_ref, k_ref, v_ref, w_ref, gains_ref):
    core, shard = ids_ref[0], ids_ref[1]
    rows = own_ref.shape[0]
    size = rows // 2
    fill(w_ref, core, shard, own_ref[...], first_ref[...], second_ref[...], size)
    columns = gain_ref[...].T[:rows]
    gains_ref[pl.ds(shard * rows, rows), :] = columns[:, 0:8]
    gains_ref[pl.ds((1 - shard) * rows, rows), :] = columns[:, 8:16]
    count = x_ref.shape[1]
    gain = gains_ref[:, 0:1]
    width_q = q_ref.shape[0]
    width_k = k_ref.shape[0]
    for at in range(0, count, BLOCK):
        cols = slice(at, at + BLOCK)
        x = x_ref[:, cols].astype(F32)
        r = lax.rsqrt(jnp.mean(x * x, axis=0, keepdims=True) + EPS)
        n = (x * r * gain).astype(BF)
        n_ref[:, cols] = n
        y = tn(w_ref[...], n)
        c = cos_ref[:, cols]
        s = sin_ref[:, cols]
        cq, sq = c * 0.125, s * 0.125
        for head in range((width_q + width_k) // HEAD_SIZE):
            row = head * HEAD_SIZE
            u1 = y[row : row + HALF]
            u2 = y[row + HALF : row + HEAD_SIZE]
            if row < width_q:
                q_ref[row : row + HALF, cols] = (u1 * cq - u2 * sq).astype(BF)
                q_ref[row + HALF : row + HEAD_SIZE, cols] = (u2 * cq + u1 * sq).astype(BF)
            else:
                row -= width_q
                k_ref[row : row + HALF, cols] = (u1 * c - u2 * s).astype(BF)
                k_ref[row + HALF : row + HEAD_SIZE, cols] = (u2 * c + u1 * s).astype(BF)
        v_ref[:, cols] = y[width_q + width_k :].astype(BF)


def causal(s):
    low = s.shape[0] - BLOCK
    rows = lax.broadcasted_iota(jnp.int32, (BLOCK, BLOCK), 0)
    cols = lax.broadcasted_iota(jnp.int32, (BLOCK, BLOCK), 1)
    keep = jnp.concatenate([rows <= cols] * (s.shape[1] // BLOCK), axis=1)
    last = jnp.where(keep, s[low:], -1e30)
    return last if low == 0 else jnp.concatenate([s[:low], last], axis=0)


def beside(ref, cols):
    return jnp.concatenate(
        [ref[h * HEAD_SIZE : (h + 1) * HEAD_SIZE, cols] for h in range(GROUP)], axis=1
    )


def attend_kernel(q_ref, k_ref, v_ref, o_ref, lse_ref):
    count = q_ref.shape[1]
    keys = k_ref[...].astype(F32).T.astype(BF)
    for at in range(0, count, BLOCK):
        end = at + BLOCK
        cols = slice(at, end)
        s = causal(nn(keys[:end], beside(q_ref, cols)))
        top = jnp.max(s, axis=0, keepdims=True)
        p = jnp.exp(s - top)
        total = jnp.sum(p, axis=0, keepdims=True)
        o = nn(v_ref[:, :end], p.astype(BF)) / total
        lse = top + jnp.log(total)
        for h in range(GROUP):
            part = slice(h * BLOCK, (h + 1) * BLOCK)
            o_ref[h * HEAD_SIZE : (h + 1) * HEAD_SIZE, cols] = o[:, part].astype(BF)
            lse_ref[h : h + 1, cols] = lse[:, part]


def middle_kernel(ids_ref, x_ref, h0_ref, h1_ref, h2_ref, own_ref, first_ref, second_ref, gain_ref, mid_ref, n_ref, w_ref, heads_ref):
    core, shard = ids_ref[0], ids_ref[1]
    rows, width = own_ref.shape
    size = rows // 2
    w_ref[pl.ds(shard * rows, rows), :] = own_ref[...]
    for ref, side in ((first_ref, core), (second_ref, 1 - core)):
        at = (1 - shard) * rows + side * size
        for i in range(-(-width // BLOCK)):
            end = min((i + 1) * BLOCK, width)
            w_ref[pl.ds(at, size), i * BLOCK : end] = ref[(6 + i) * size : (7 + i) * size, : end - i * BLOCK]
    heads_ref[...] = jnp.concatenate([h0_ref[...], h1_ref[...], h2_ref[...]], axis=0)
    count = x_ref.shape[1]
    gain = gain_ref[:, 1:2]
    for at in range(0, count, BLOCK):
        cols = slice(at, at + BLOCK)
        m = x_ref[:, cols].astype(F32) + tn(w_ref[...], heads_ref[:, cols])
        r = lax.rsqrt(jnp.mean(m * m, axis=0, keepdims=True) + EPS)
        mid_ref[:, cols] = m
        n_ref[:, cols] = (m * r * gain).astype(BF)


def norm_back(x, gain, grad):
    r = lax.rsqrt(jnp.mean(x * x, axis=0, keepdims=True) + EPS)
    scaled = gain * grad
    dot = jnp.mean(scaled * x, axis=0, keepdims=True)
    return r * scaled - x * (r * r * r * dot)


def put(refs, ids_ref, half, shard, lane_half, rows, value):
    core = ids_ref[0]
    keep_ref, send_ref = refs
    s, y = flip(ids_ref[1], shard), flip(ids_ref[2], lane_half)
    one, two = jnp.where(core == 0, s, y), jnp.where(core == 0, y, s)

    @pl.when(core == half)
    def _():
        keep_ref[one, two, rows] = value

    @pl.when(core != half)
    def _():
        send_ref[two, one, rows] = value


def mlp_block(b, ids_ref, n_ref, cot_ref, wg_ref, wu_ref, wd_ref, first_ref, second_ref,
              acc_in, gn_in, refs, acc_ref, gn_ref, w, wd, act):
    core, shard = ids_ref[0], ids_ref[1]
    rows = wg_ref.shape[0]
    size = rows // 2
    hid = 2 * BLOCK
    blocks = wd_ref.shape[1] // BLOCK
    for i in range(4):
        part = slice(i * size, (i + 1) * size)
        own = (wg_ref, wu_ref)[i // 2][:, (i % 2 * blocks + b) * BLOCK : (i % 2 * blocks + b + 1) * BLOCK]
        fill(w.at[:, i * BLOCK : (i + 1) * BLOCK], core, shard, own, first_ref[part], second_ref[part], size)
    for s in range(2):
        cols = slice(s * BLOCK, (s + 1) * BLOCK)

        @pl.when(shard == s)
        def _():
            wd[:, cols] = wd_ref[:, b * BLOCK : (b + 1) * BLOCK]

        @pl.when(shard != s)
        def _():
            wd[pl.ds(core * rows, rows), cols] = first_ref[4 * size : 6 * size]
            wd[pl.ds((1 - core) * rows, rows), cols] = second_ref[4 * size : 6 * size]

    count = n_ref.shape[1]
    for at in range(0, count, BLOCK):
        cols = slice(at, at + BLOCK)
        both = tn(w[...], n_ref[:, cols])
        gate, up = both[:hid], both[hid:]
        gh = tn(wd[...], cot_ref[:, cols])
        sig = 0.5 * jnp.tanh(0.5 * gate) + 0.5
        a = gate * sig
        act[:hid, cols] = (a * up).astype(BF)
        act[hid : 2 * hid, cols] = (gh * up * (sig + a * (1.0 - sig))).astype(BF)
        act[2 * hid :, cols] = (gh * a).astype(BF)
        part = nn(wd[...], act[:hid, cols])
        gpart = nn(w[...], act[hid:, cols])
        acc_ref[:, cols] = part if acc_in is None else acc_in[:, cols] + part
        gn_ref[:, cols] = gpart if gn_in is None else gn_in[:, cols] + gpart
    for s in range(2):
        gd = nt(cot_ref[...], act[s * BLOCK : (s + 1) * BLOCK]).astype(BF)
        gg = nt(n_ref[...], act[hid + s * BLOCK : hid + (s + 1) * BLOCK]).astype(BF)
        gu = nt(n_ref[...], act[2 * hid + s * BLOCK : 2 * hid + (s + 1) * BLOCK]).astype(BF)
        for z in range(2):
            lanes = slice(z * LANES, (z + 1) * LANES)
            for half in range(2):
                part = slice(half * rows, (half + 1) * rows)
                put(refs, ids_ref, half, s, z, slice(0, rows), gd[part, lanes])
                put(refs, ids_ref, s, half, z, slice(rows, 2 * rows), gg[part, lanes])
                put(refs, ids_ref, s, half, z, slice(2 * rows, 3 * rows), gu[part, lanes])


def mlp_one_kernel(b, ids_ref, n_ref, cot_ref, wg, wu, wd, first, second, keep, send, acc, gn, *scratch):
    mlp_block(b, ids_ref, n_ref, cot_ref, wg, wu, wd, first, second, None, None, (keep, send), acc, gn, *scratch)


def mlp_two_kernel(b, ids_ref, n_ref, cot_ref, wg, wu, wd, first, second, acc_in, gn_in,
                   keep, send, acc, gn, *scratch):
    mlp_block(b, ids_ref, n_ref, cot_ref, wg, wu, wd, first, second, acc_in, gn_in, (keep, send), acc, gn, *scratch)


def between_kernel(ids_ref, cot_ref, acc, gn, mid_ref, gain_ref, heads_ref, wo_ref,
                   keep, send, out_ref, gmid_ref, gheads_ref):
    width, count = cot_ref.shape
    gain = gain_ref[:, 1:2]
    low = []
    for at in range(0, count, BLOCK):
        cols = slice(at, at + BLOCK)
        mid = mid_ref[:, cols]
        out_ref[:, cols] = (mid + acc[:, cols]).astype(BF)
        gm = cot_ref[:, cols].astype(F32) + norm_back(mid, gain, gn[:, cols])
        gmid_ref[:, cols] = gm
        low.append(gm.astype(BF))
        gheads_ref[:, cols] = nn(wo_ref[...], low[-1]).astype(BF)
    g = nt(heads_ref[...], jnp.concatenate(low, axis=1)).astype(BF)
    per = -(-(-(-width // LANES)) // 2)
    size = width // 4
    base = 0
    rest = keep.shape[2] - per * size
    for s in range(2):
        for half in range(2):
            rows = slice((2 * s + half) * size, (2 * s + half + 1) * size)
            for i in range(2 * per):
                end = min((i + 1) * LANES, width)
                value = g[rows, i * LANES : end] if end > i * LANES else None
                if value is None:
                    value = jnp.zeros((size, LANES), BF)
                elif end < (i + 1) * LANES:
                    value = jnp.concatenate([value, jnp.zeros((size, (i + 1) * LANES - end), BF)], axis=1)
                at = base + (i % per) * size
                put((keep, send), ids_ref, half, s, i // per, slice(at, at + size), value)
            if rest:
                for y in range(2):
                    put((keep, send), ids_ref, half, s, y, slice(base + per * size, base + per * size + rest),
                        jnp.zeros((rest, LANES), BF))


def attend_back_kernel(q_ref, k_ref, v_ref, o_ref, lse_ref, go_ref, cos_ref, sin_ref,
                       gq_ref, gk_ref, gv_ref, dk_ref, dv_ref):
    count = q_ref.shape[1]
    keys = k_ref[...].astype(F32).T.astype(BF)
    values = v_ref[...].astype(F32).T.astype(BF)
    dk_ref[...] = jnp.zeros_like(dk_ref)
    dv_ref[...] = jnp.zeros_like(dv_ref)
    for at in range(0, count, BLOCK):
        end = at + BLOCK
        cols = slice(at, end)
        q = beside(q_ref, cols)
        go = beside(go_ref, cols)
        delta = jnp.sum(go.astype(F32) * beside(o_ref, cols).astype(F32), axis=0, keepdims=True)
        lse = jnp.concatenate([lse_ref[h : h + 1, cols] for h in range(GROUP)], axis=1)
        s = causal(nn(keys[:end], q))
        p = jnp.exp(s - lse)
        ds = (p * (nn(values[:end], go) - delta)).astype(BF)
        dv_ref[:, :end] += nt(go, p.astype(BF))
        dk_ref[:, :end] += nt(q, ds)
        dq = nn(k_ref[:, :end], ds)
        c = cos_ref[:, cols] * 0.125
        sn = sin_ref[:, cols] * 0.125
        for h in range(GROUP):
            part = slice(h * BLOCK, (h + 1) * BLOCK)
            g1, g2 = dq[:HALF, part], dq[HALF:, part]
            row = h * HEAD_SIZE
            gq_ref[row : row + HALF, cols] = (g1 * c + g2 * sn).astype(BF)
            gq_ref[row + HALF : row + HEAD_SIZE, cols] = (g2 * c - g1 * sn).astype(BF)
    c = cos_ref[...]
    sn = sin_ref[...]
    g1, g2 = dk_ref[:HALF], dk_ref[HALF:]
    gk_ref[:HALF] = (g1 * c + g2 * sn).astype(BF)
    gk_ref[HALF:] = (g2 * c - g1 * sn).astype(BF)
    gv_ref[...] = dv_ref[...].astype(BF)


def weight_kernel(ids_ref, n_ref, *refs):
    count = (len(refs) - 2) // 3
    keep_ref, send_ref = refs[-2:]
    size, lanes = keep_ref.shape[2:]
    g = jnp.concatenate([refs[i * count + j][...] for i in range(3) for j in range(count)], axis=0)
    wide = g.shape[0]
    for z in range(2):
        end = min((z + 1) * lanes, wide)
        w = nt(n_ref[...], g[z * lanes : end]).astype(BF)
        if end < (z + 1) * lanes:
            w = jnp.concatenate([w, jnp.zeros((w.shape[0], (z + 1) * lanes - end), BF)], axis=1)
        for s in range(2):
            for half in range(2):
                at = (2 * s + half) * size
                put((keep_ref, send_ref), ids_ref, half, s, z, slice(0, size), w[at : at + size])


def tokens_kernel(x_ref, gain_ref, w_ref, gmid_ref, *refs):
    out_ref = refs[-1]
    parts = (len(refs) - 1) // 3
    count = x_ref.shape[1]
    gain = gain_ref[:, 0:1]
    for at in range(0, count, BLOCK):
        cols = slice(at, at + BLOCK)
        g = jnp.concatenate([refs[i * parts + j][:, cols] for i in range(3) for j in range(parts)], axis=0)
        gn = nn(w_ref[...], g)
        x = x_ref[:, cols].astype(F32)
        out_ref[:, cols] = (gmid_ref[:, cols] + norm_back(x, gain, gn)).astype(BF)


def plus(a, b):
    return (a.astype(F32) + b.astype(F32)).astype(BF)


def add_first_kernel(*refs):
    count = (len(refs) - 2) // 2
    send_ref, keep_ref = refs[-2:]
    at = 0
    for i in range(count):
        a, b = refs[i], refs[count + i]
        rows = slice(at, at + a.shape[2])
        at += a.shape[2]
        for j in range(2):
            send_ref[j, rows] = plus(a[1, j], b[1, j])
            keep_ref[j, rows] = plus(a[0, j], b[0, j])


def add_second_kernel(a_ref, b_ref, send_ref, keep_ref):
    send_ref[...] = plus(a_ref[1], b_ref[1])
    keep_ref[...] = plus(a_ref[0], b_ref[0])


def add_split_kernel(ids_ref, a_ref, b_ref, send_ref, keep_ref):
    z = ids_ref[3]
    rows = send_ref.shape[0]
    for ref, side in ((send_ref, 1 - z), (keep_ref, z)):
        part = pl.ds(side * rows, rows)
        ref[...] = plus(a_ref[part, :], b_ref[part, :])


def add_kernel(a_ref, b_ref, out_ref):
    out_ref[...] = plus(a_ref[...], b_ref[...])


def join_kernel(ids_ref, a_ref, b_ref, out_ref):
    z = ids_ref[3]
    rows = a_ref.shape[0]
    out_ref[pl.ds(z * rows, rows), :] = a_ref[...]
    out_ref[pl.ds((1 - z) * rows, rows), :] = b_ref[...]


def chosen(ids_ref, refs, half, y, rows):
    core, side = ids_ref[0], ids_ref[2]
    own, own_other, far, far_other = (ref[rows] for ref in refs)
    near = jnp.where(side == y, own, own_other)
    return jnp.where(core == half, near, jnp.where(side == y, far, far_other)).astype(F32)


def as_row(column_sums):
    rows = column_sums.shape[0]
    padded = -(-rows // LANES) * LANES
    if padded > rows:
        column_sums = jnp.concatenate([column_sums, jnp.zeros((padded - rows, LANES), F32)], axis=0)
    return jnp.sum(column_sums.T, axis=0, keepdims=True)[:, :rows]


def finish_first_kernel(ids_ref, a0, a1, a2, a3, wg_ref, wu_ref, gate_ref, up_ref, down_ref, total_ref):
    rows, ff = gate_ref.shape
    blocks = ff // 2 // BLOCK
    total = jnp.zeros((rows, LANES), F32)
    for b in range(blocks - 1):
        for z in range(2):
            for half in range(2):
                base = 3 * b * rows
                at = b * BLOCK + z * LANES
                down_ref[half * rows : (half + 1) * rows, at : at + LANES] = chosen(
                    ids_ref, (a0, a1, a2, a3), half, z, slice(base, base + rows))
                at += half * blocks * BLOCK
                for i, w_ref, to in ((1, wg_ref, gate_ref), (2, wu_ref, up_ref)):
                    g = chosen(ids_ref, (a0, a1, a2, a3), half, z, slice(base + i * rows, base + (i + 1) * rows))
                    to[:, at : at + LANES] = g
                    total += g * w_ref[:, at : at + LANES].astype(F32)
    total_ref[...] = total


def finish_last_kernel(ids_ref, b0, b1, b2, b3, wg_ref, wu_ref, total_in, gain_ref, gate_in, up_in, down_in,
                       gate_ref, up_ref, down_ref, out_ref, gain_out_ref, total_ref):
    half = pl.program_id(0)
    rows = gate_ref.shape[0]
    refs = (b0, b1, b2, b3)
    total = jnp.zeros((rows, LANES), F32)
    for z in range(2):
        lanes = slice(z * LANES, (z + 1) * LANES)
        down_ref[pl.ds(half * rows, rows), lanes] = chosen(ids_ref, refs, half, z, slice(0, rows))
        for i, w_ref, to in ((1, wg_ref, gate_ref), (2, wu_ref, up_ref)):
            g = chosen(ids_ref, refs, half, z, slice(i * rows, (i + 1) * rows))
            to[:, lanes] = g
            total += g * w_ref[:, lanes].astype(F32)

    @pl.when(half == 0)
    def _():
        total_ref[...] = total_in[...] + total

    @pl.when(half == 1)
    def _():
        gain_out_ref[...] = as_row(total_ref[...] + total) / gain_ref[1:2, :rows]
        width = out_ref.shape[1]
        pieces = -(-width // LANES)
        per = -(-pieces // 2)
        size = rows // 2
        for part in range(2):
            for i in range(pieces):
                end = min((i + 1) * LANES, width)
                at = 3 * rows + (i % per) * size
                g = chosen(ids_ref, refs, part, i // per, slice(at, at + size))
                out_ref[part * size : (part + 1) * size, i * LANES : end] = g[:, : end - i * LANES]


def finish_qkv_kernel(ids_ref, a0, a1, a2, a3, w_ref, gain_ref, q_ref, k_ref, v_ref, gain_out_ref, sum_ref):
    size, lanes = a0.shape
    wide_q, wide_k = q_ref.shape[1], k_ref.shape[1]
    wide = w_ref.shape[1]
    for half in range(2):
        rows = slice(half * size, (half + 1) * size)
        parts = [chosen(ids_ref, (a0, a1, a2, a3), half, z, slice(0, size)) for z in range(2)]
        g = jnp.concatenate(parts, axis=1)[:, :wide]
        q_ref[rows] = g[:, :wide_q]
        k_ref[rows] = g[:, wide_q : wide_q + wide_k]
        v_ref[rows] = g[:, wide_q + wide_k :]
        sums = jnp.sum(g * w_ref[rows].astype(F32), axis=1, keepdims=True)
        sum_ref[rows] = sums * (lax.broadcasted_iota(jnp.int32, (size, LANES), 1) == 0).astype(F32)
    gain_out_ref[...] = as_row(sum_ref[...]) / gain_ref[0:1, : gain_out_ref.shape[1]]


class Grid:
    def __init__(self, shards, replicas):
        self.shards, self.replicas = shards, replicas
        self.shard = lax.axis_index("shard")
        self.replica = lax.axis_index("replica")
        self.rest = [1 << i for i in range(3, replicas.bit_length() - 1)]
        self.ids = jnp.stack(
            [self.side(CORE), self.shard, self.side(SIDE), self.side(SPLIT)]
        ).astype(jnp.int32)

    def side(self, bit):
        return (self.replica // bit) % 2

    def swap(self, a, even, odd=None):
        odd = even if odd is None else odd
        pairs = []
        for s in range(self.shards):
            for r in range(self.replicas):
                shard, bit = odd if r % 2 else even
                pairs.append((s * self.replicas + r, (s ^ shard) * self.replicas + (r ^ bit)))
        return lax.ppermute(a, AXES, pairs)


def tie(values, others):
    return lax.optimization_barrier((tuple(values), tuple(others)))[0]


def flow(grid, keeps, sends, gots, split):
    rows = sum(k.shape[2] for k in keeps)
    lanes = keeps[0].shape[3]
    ops = 10**4
    after = yield sends
    gots = tie(gots, after)
    two = shape(2, rows, lanes)
    send, keep = call(add_first_kernel, "add_core", [two, two], ops,
                      in_specs=[whole()] * (2 * len(keeps)), out_specs=[whole()] * 2)(*keeps, *gots)
    got = grid.swap(send, (1, 0), (0, SIDE))
    after = yield [send]
    (got,) = tie([got], after)
    one = shape(rows, lanes)
    send, keep = call(add_second_kernel, "add_second", [one, one], ops,
                      in_specs=[whole()] * 2, out_specs=[whole()] * 2)(keep, got)
    got = grid.swap(send, (0, SIDE), (1, 0))
    after = yield [send]
    (got,) = tie([got], after)

    def add(a, b):
        return call(add_kernel, "add", shape(*a.shape), ops, in_specs=[whole()] * 2, out_specs=whole())(a, b)

    if split:
        half = shape(rows // 2, lanes)
        send, keep = call(add_split_kernel, "add_split", [half, half], ops,
                          in_specs=[smem()] + [whole()] * 2, out_specs=[whole()] * 2)(grid.ids, keep, got)
    else:
        send = keep = add(keep, got)
    got = grid.swap(send, (0, SPLIT))
    after = yield [send]
    (got,) = tie([got], after)
    a = add(keep, got)
    for bit in grid.rest[1:]:
        a = add(a, grid.swap(a, (0, bit)))
    got = grid.swap(a, (0, grid.rest[0]))
    after = yield [a]
    (got,) = tie([got], after)
    a = add(a, got)
    if split:
        got = grid.swap(a, (0, SPLIT))
        after = yield [a]
        (got,) = tie([got], after)
        a = call(join_kernel, "join", one, ops, in_specs=[smem()] + [whole()] * 2, out_specs=whole())(grid.ids, a, got)
    b = grid.swap(a, (0, SIDE))
    far = grid.swap(a, (0, CORE))
    after = yield [a]
    (b,) = tie([b], after)
    far_b = grid.swap(b, (0, CORE))
    yield a, b, far, far_b


def local(shards, replicas, tokens, cotangent, lengths, attn_gain, w_query, key_projection,
          value_projection, w_out, mlp_gain, w_gate, w_up, w_down):
    grid = Grid(shards, replicas)
    ids = grid.ids
    count, width = tokens.shape
    rows = w_query.shape[0]
    size = rows // 2
    ff = w_gate.shape[1]
    blocks = ff // 2 // BLOCK
    wide_k = key_projection.shape[1]
    wide = width + 2 * wide_k
    x = tokens.T
    cot = cotangent.T
    cos, sin = tables(count)
    own_down = w_down.T
    padded = -(-rows // LANES) * LANES
    other_one, other_two = grid.swap(attn_gain, (1, 0)), grid.swap(mlp_gain, (1, 0))
    none = jnp.zeros((6, rows), BF)
    gain_rows = jnp.concatenate([attn_gain[None], mlp_gain[None], none, other_one[None], other_two[None], none])
    gain_rows = jnp.pad(gain_rows.astype(F32), ((0, 0), (0, padded - rows)))

    own_qkv, half_qkv = call(
        pack_first_kernel, "pack_first", [shape(rows, wide), shape(size, wide)], 10**6, grid=(1,), limit=60,
        in_specs=[smem(), copied(rows, width), copied(rows, wide_k), copied(rows, wide_k)],
        out_specs=[copied(rows, wide), copied(size, wide)],
    )(ids, w_query, key_projection, value_projection)
    first_qkv = grid.swap(half_qkv, (1, 0))

    tall = [(6 + (-(-width // BLOCK) if b == 0 else 0)) * size for b in range(blocks)]
    (w_gate_,) = tie([w_gate], [half_qkv])
    pack_a, pack_b, pack_c = call(
        pack_kernel, "pack", [shape(t, BLOCK) for t in tall], 10**6, grid=(1,), limit=60,
        in_specs=[smem(), copied(rows, ff), copied(rows, ff), copied(width, ff // 2), copied(rows, width)],
        out_specs=[copied(t, BLOCK) for t in tall],
    )(ids, w_gate_, w_up, own_down, w_out)
    first_a = grid.swap(pack_a, (1, 0))
    (first_qkv,) = tie([first_qkv], [pack_a])
    second_qkv = grid.swap(first_qkv, (0, CORE))

    normed, q, k, v, w_qkv, gains = call(
        qkv_kernel, "qkv",
        [shape(width, count), shape(width, count), shape(wide_k, count), shape(wide_k, count), shape(width, wide),
         shape(width, 8, dtype=F32)],
        2 * count * width * wide, in_specs=[smem()] + [whole()] * 7, out_specs=[whole()] * 6,
    )(ids, x, gain_rows, own_qkv, first_qkv, second_qkv, cos, sin)
    first_b = grid.swap(tie([pack_b], [q])[0], (1, 0))

    group = GROUP * HEAD_SIZE

    def of_group(g):
        block_q = pl.BlockSpec((group, count), lambda i: (g, 0))
        return block_q, pl.BlockSpec((HEAD_SIZE, count), lambda i: (g, 0))

    heads, lse = [], []
    q_ = q
    for g in range(KEY_VALUE_HEADS):
        block_q, block_k = of_group(g)
        o, l = call(
            attend_kernel, "attend", [shape(group, count), shape(8, count, dtype=F32)], 8 * count * count * group,
            grid=(1,), in_specs=[block_q, block_k, block_k], out_specs=[copied(group, count), copied(8, count)], limit=20,
        )(q_, k, v)
        heads.append(o)
        lse.append(l)
        (q_,) = tie([q], [o])
    first_c = grid.swap(tie([pack_c], heads[:1])[0], (1, 0))
    (first_a,) = tie([first_a], heads)
    second_a = grid.swap(first_a, (0, CORE))

    middle, normed_two, w_o, all_heads = call(
        middle_kernel, "middle",
        [shape(width, count, dtype=F32), shape(width, count), shape(width, width), shape(width, count)],
        2 * count * width * width, in_specs=[smem()] + [whole()] * 8, out_specs=[whole()] * 4,
    )(ids, x, *heads, w_out, first_a, second_a, gains)

    scratch = [pltpu.VMEM((width, 4 * BLOCK), BF), pltpu.VMEM((width, 2 * BLOCK), BF), pltpu.VMEM((6 * BLOCK, count), BF)]
    float_act = shape(width, count, dtype=F32)

    def mlp(kernel, b, outs, first, second, more):
        return call(
            functools.partial(kernel, b), "mlp", outs, 18 * count * width * ff // blocks,
            in_specs=[smem()] + [whole()] * (7 + len(more)), out_specs=[whole()] * len(outs),
            scratch=scratch, limit=24, weight=10,
        )(ids, normed_two, cot, w_gate, w_up, own_down, first, second, *more)

    part = (2, 2, 3 * rows, LANES)
    keep_a, send_a, acc, gn = mlp(mlp_one_kernel, 0, [shape(*part)] * 2 + [float_act] * 2, first_a, second_a, [])
    (first_b,) = tie([first_b], [acc])
    second_b = grid.swap(first_b, (0, CORE))
    got_a = grid.swap(send_a, (0, CORE))
    keep_b, send_b, acc, gn = mlp(
        mlp_two_kernel, 1, [shape(*part)] * 2 + [float_act] * 2, first_b, second_b, [acc, gn])
    got_b = grid.swap(send_b, (0, CORE))
    (first_c,) = tie([first_c], [acc])
    second_c = grid.swap(first_c, (0, CORE))
    keep_c, send_c, acc, gn = mlp(
        mlp_two_kernel, 2, [shape(*part)] * 2 + [float_act] * 2, first_c, second_c, [acc, gn])
    got_c = grid.swap(send_c, (0, CORE))
    flows = {"a": flow(grid, [keep_a, keep_b], [send_a, send_b], [got_a, got_b], True)}
    next(flows["a"])
    sums = {}
    state = {"after": [acc]}

    def step(names):
        for name in names:
            sent = flows[name].send(state["after"])
            if len(sent) == 4:
                sums[name] = sent
            else:
                state["after"] = sent

    def then(value):
        return tie([value], state["after"])[0]

    step("a")
    per = -(-(-(-width // LANES)) // 2)
    part_o = (2, 2, -(-per * size // 32) * 32, LANES)
    keep_o, send_o, out, g_mid, g_heads = call(
        between_kernel, "between",
        [shape(*part_o), shape(*part_o), shape(width, count), float_act, shape(width, count)],
        4 * count * width * width, in_specs=[smem()] + [whole()] * 7, out_specs=[whole()] * 5, limit=24, weight=10,
    )(ids, then(cot), acc, gn, middle, gains, all_heads, w_o)
    flows["b"] = flow(grid, [keep_c, keep_o], [send_c, send_o], [got_c, grid.swap(send_o, (0, CORE))], True)
    next(flows["b"])
    state["after"] = [g_heads]

    grads = []
    for g, name in enumerate(("ba", "", "ba")):
        block_q, block_k = of_group(g)
        out_q, out_k = copied(group, count), copied(HEAD_SIZE, count)
        grads.append(call(
            attend_back_kernel, "attend_back", [shape(group, count), shape(HEAD_SIZE, count), shape(HEAD_SIZE, count)],
            4 * count * count * width, grid=(1,),
            in_specs=[block_q, block_k, block_k, out_q, copied(8, count), block_q] + [copied(HALF, count)] * 2,
            out_specs=[out_q, out_k, out_k],
            scratch=[pltpu.VMEM((HEAD_SIZE, count), F32)] * 2, limit=24, weight=10 if g == 0 else 1,
        )(q, k, v, heads[g], lse[g], then(g_heads), cos, sin))
        state["after"] = [grads[-1][2]]
        step(name)
    grads = [g[i] for i in range(3) for g in grads]

    lanes = -(-wide // (2 * LANES)) * LANES
    part_three = (2, 2, size, lanes)
    keep_d, send_d = call(
        weight_kernel, "weights", [shape(*part_three), shape(*part_three)], 2 * count * width * wide,
        in_specs=[smem()] + [whole()] * 10, out_specs=[whole()] * 2,
    )(ids, then(normed), *grads)
    flows["d"] = flow(grid, [keep_d], [send_d], [grid.swap(send_d, (0, CORE))], False)
    next(flows["d"])
    state["after"] = [send_d]
    step("dab")
    grad_tokens = call(
        tokens_kernel, "grad_tokens", shape(width, count), 2 * count * width * wide,
        in_specs=[whole()] * 13, out_specs=whole(),
    )(then(x), gains, w_qkv, g_mid, *grads)
    state["after"] = [grad_tokens]
    step("dbdadbadbad")
    g_gate, g_up, g_down, partial = call(
        finish_first_kernel, "finish_first",
        [shape(rows, ff, dtype=F32), shape(rows, ff, dtype=F32), shape(width, ff // 2, dtype=F32),
         shape(rows, LANES, dtype=F32)],
        10**7, in_specs=[smem()] + [whole()] * 6, out_specs=[whole()] * 4,
    )(ids, *sums["a"], then(w_gate), w_up)
    g_query, g_key, g_value, g_gain_one = call(
        finish_qkv_kernel, "finish_qkv",
        [shape(rows, width, dtype=F32), shape(rows, wide_k, dtype=F32), shape(rows, wide_k, dtype=F32),
         shape(1, rows, dtype=F32)],
        10**7, in_specs=[smem()] + [whole()] * 6, out_specs=[whole()] * 4, scratch=[pltpu.VMEM((rows, LANES), F32)],
    )(ids, *sums["d"], tie([own_qkv], [partial])[0], gain_rows)
    state["after"] = [partial]
    step("b")
    piece = pl.BlockSpec((rows, BLOCK), lambda i: (0, (i + 1) * blocks - 1))
    last = pl.BlockSpec((width, BLOCK), lambda i: (0, blocks - 1))
    kept = pl.BlockSpec(memory_space=pl.ANY)
    tall = sums["b"][0].shape
    g_gate, g_up, g_down, g_out, g_gain_two = call(
        finish_last_kernel, "finish_last",
        [shape(rows, ff, dtype=F32), shape(rows, ff, dtype=F32), shape(width, ff // 2, dtype=F32),
         shape(rows, width, dtype=F32), shape(1, rows, dtype=F32)],
        10**7, grid=(2,),
        in_specs=[smem()] + [copied(*tall)] * 4 + [piece, piece, copied(rows, LANES), copied(16, padded)] + [kept] * 3,
        out_specs=[piece, piece, last, copied(rows, width), copied(1, rows)],
        scratch=[pltpu.VMEM((rows, LANES), F32)], aliases={9: 0, 10: 1, 11: 2},
    )(ids, *sums["b"], w_gate, w_up, partial, gain_rows, g_gate, g_up, g_down)
    return (
        out.T,
        grad_tokens.T,
        g_gain_one[0],
        g_query,
        g_key,
        g_value,
        g_out,
        g_gain_two[0],
        g_gate,
        g_up,
        g_down.T,
    )


def solution(mesh):
    tokens = P(AXES, None)
    split = P("shard", None)
    gain = P("shard")
    return jax.shard_map(
        functools.partial(local, mesh.shape["shard"], mesh.shape["replica"]),
        mesh=mesh,
        in_specs=(tokens, tokens, tokens, gain, split, split, split, split, gain, split, split, split),
        out_specs=(tokens, tokens, gain, split, split, split, split, gain, split, split, split),
        check_vma=False,
    )
```

```python
import functools
import math

import jax
import jax.numpy as jnp
import numpy as np
from jax import lax
from jax.experimental import pallas as pl
from jax.experimental.pallas import tpu as pltpu
from jax.sharding import PartitionSpec as P

QUERY_HEADS = 9
KEY_VALUE_HEADS = 3
HEAD_SIZE = 64
HALF = HEAD_SIZE // 2
GROUP = QUERY_HEADS // KEY_VALUE_HEADS
EPS = 1e-05
THETA = 100000.0
BF = jnp.bfloat16
F32 = jnp.float32
BLOCK = 256
AXES = ("shard", "replica")
LANES = 128
TIMES = dict(pack_first=2, pack=3, qkv=3.6, attend=3, middle=2.2, mlp=9, between=5.5, attend_back=5, weights=2.4,
             grad_tokens=3.5, finish_first=3.7, finish_qkv=2, finish_last=2.6, add_core=0.4, add_second=0.4,
             add_split=0.5, add=0.3, join=0.6, pause=10)
CORE, SIDE, SPLIT = 1, 2, 4


def nn(a, b):
    return lax.dot_general(a, b, (((1,), (0,)), ((), ())), preferred_element_type=F32)


def nt(a, b):
    return lax.dot_general(a, b, (((1,), (1,)), ((), ())), preferred_element_type=F32)


def tn(a, b):
    return lax.dot_general(a, b, (((0,), (0,)), ((), ())), preferred_element_type=F32)


def whole():
    return pl.BlockSpec(memory_space=pltpu.VMEM)


def call(kernel, name, outs, flops, grid=None, in_specs=None, out_specs=None, scratch=(), limit=16, weight=1, aliases=None):
    return pl.pallas_call(
        kernel,
        name=name,
        out_shape=outs,
        grid=grid or (),
        in_specs=in_specs,
        out_specs=out_specs,
        scratch_shapes=list(scratch),
        compiler_params=pltpu.CompilerParams(vmem_limit_bytes=limit * 2**20),
        input_output_aliases=aliases or {},
        cost_estimate=pl.CostEstimate(flops=int(TIMES[name] * 0.46 * 10**9), bytes_accessed=1024, transcendentals=0),
    )


def copied(*dims):
    return pl.BlockSpec(dims, lambda i: (0,) * len(dims))


def shape(*dims, dtype=BF):
    return jax.ShapeDtypeStruct(dims, dtype)


def tables(count):
    inverse = np.exp(np.arange(HALF, dtype=np.float32) * np.float32(-2.0 * math.log(THETA) / HEAD_SIZE))
    angles = jnp.arange(count, dtype=jnp.int32).astype(F32)[None, :] * jnp.asarray(inverse)[:, None]
    return jnp.cos(angles), jnp.sin(angles)

def smem():
    return pl.BlockSpec(memory_space=pltpu.SMEM)


def flip(a, b):
    return lax.rem(a + b, 2)


def pack_first_kernel(ids_ref, wq_ref, wk_ref, wv_ref, own_ref, half_ref):
    size = half_ref.shape[0]
    own_ref[...] = jnp.concatenate([wq_ref[...], wk_ref[...], wv_ref[...]], axis=1)
    half_ref[...] = own_ref[pl.ds(ids_ref[0] * size, size), :]


def pack_kernel(ids_ref, wg_ref, wu_ref, wd_ref, wo_ref, *out_refs):
    core = ids_ref[0]
    rows, width = wo_ref.shape
    size = rows // 2
    mine = pl.ds(core * size, size)
    blocks = len(out_refs)
    for b, out_ref in enumerate(out_refs):
        for s in range(2):
            cols = slice((s * blocks + b) * BLOCK, (s * blocks + b + 1) * BLOCK)
            out_ref[s * size : (s + 1) * size, :] = wg_ref[mine, cols]
            out_ref[(2 + s) * size : (3 + s) * size, :] = wu_ref[mine, cols]
        out_ref[4 * size : 6 * size, :] = wd_ref[pl.ds(core * rows, rows), b * BLOCK : (b + 1) * BLOCK]
    for i in range(-(-width // BLOCK)):
        end = min((i + 1) * BLOCK, width)
        piece = wo_ref[mine, i * BLOCK : end]
        if end < (i + 1) * BLOCK:
            piece = jnp.concatenate([piece, jnp.zeros((size, (i + 1) * BLOCK - end), BF)], axis=1)
        out_refs[0][(6 + i) * size : (7 + i) * size, :] = piece


def fill(to, core, shard, own, first, second, size):
    rows = 2 * size
    to[pl.ds(shard * rows, rows), :] = own
    to[pl.ds((1 - shard) * rows + core * size, size), :] = first
    to[pl.ds((1 - shard) * rows + (1 - core) * size, size), :] = second


def qkv_kernel(ids_ref, x_ref, gain_ref, own_ref, first_ref, second_ref, cos_ref, sin_ref,
               n_ref, q_ref, k_ref, v_ref, w_ref, gains_ref):
    core, shard = ids_ref[0], ids_ref[1]
    rows = own_ref.shape[0]
    size = rows // 2
    fill(w_ref, core, shard, own_ref[...], first_ref[...], second_ref[...], size)
    columns = gain_ref[...].T[:rows]
    gains_ref[pl.ds(shard * rows, rows), :] = columns[:, 0:8]
    gains_ref[pl.ds((1 - shard) * rows, rows), :] = columns[:, 8:16]
    count = x_ref.shape[1]
    gain = gains_ref[:, 0:1]
    width_q = q_ref.shape[0]
    width_k = k_ref.shape[0]
    for at in range(0, count, BLOCK):
        cols = slice(at, at + BLOCK)
        x = x_ref[:, cols].astype(F32)
        r = lax.rsqrt(jnp.mean(x * x, axis=0, keepdims=True) + EPS)
        n = (x * r * gain).astype(BF)
        n_ref[:, cols] = n
        y = tn(w_ref[...], n)
        c = cos_ref[:, cols]
        s = sin_ref[:, cols]
        cq, sq = c * 0.125, s * 0.125
        for head in range((width_q + width_k) // HEAD_SIZE):
            row = head * HEAD_SIZE
            u1 = y[row : row + HALF]
            u2 = y[row + HALF : row + HEAD_SIZE]
            if row < width_q:
                q_ref[row : row + HALF, cols] = (u1 * cq - u2 * sq).astype(BF)
                q_ref[row + HALF : row + HEAD_SIZE, cols] = (u2 * cq + u1 * sq).astype(BF)
            else:
                row -= width_q
                k_ref[row : row + HALF, cols] = (u1 * c - u2 * s).astype(BF)
                k_ref[row + HALF : row + HEAD_SIZE, cols] = (u2 * c + u1 * s).astype(BF)
        v_ref[:, cols] = y[width_q + width_k :].astype(BF)


def causal(s):
    low = s.shape[0] - BLOCK
    rows = lax.broadcasted_iota(jnp.int32, (BLOCK, BLOCK), 0)
    cols = lax.broadcasted_iota(jnp.int32, (BLOCK, BLOCK), 1)
    keep = jnp.concatenate([rows <= cols] * (s.shape[1] // BLOCK), axis=1)
    last = jnp.where(keep, s[low:], -1e30)
    return last if low == 0 else jnp.concatenate([s[:low], last], axis=0)


def beside(ref, cols):
    return jnp.concatenate(
        [ref[h * HEAD_SIZE : (h + 1) * HEAD_SIZE, cols] for h in range(GROUP)], axis=1
    )


def attend_kernel(q_ref, k_ref, v_ref, o_ref, lse_ref):
    count = q_ref.shape[1]
    keys = k_ref[...].astype(F32).T.astype(BF)
    for at in range(0, count, BLOCK):
        end = at + BLOCK
        cols = slice(at, end)
        s = causal(nn(keys[:end], beside(q_ref, cols)))
        top = jnp.max(s, axis=0, keepdims=True)
        p = jnp.exp(s - top)
        total = jnp.sum(p, axis=0, keepdims=True)
        o = nn(v_ref[:, :end], p.astype(BF)) / total
        lse = top + jnp.log(total)
        for h in range(GROUP):
            part = slice(h * BLOCK, (h + 1) * BLOCK)
            o_ref[h * HEAD_SIZE : (h + 1) * HEAD_SIZE, cols] = o[:, part].astype(BF)
            lse_ref[h : h + 1, cols] = lse[:, part]


def middle_kernel(ids_ref, x_ref, h0_ref, h1_ref, h2_ref, own_ref, first_ref, second_ref, gain_ref, mid_ref, n_ref, w_ref, heads_ref):
    core, shard = ids_ref[0], ids_ref[1]
    rows, width = own_ref.shape
    size = rows // 2
    w_ref[pl.ds(shard * rows, rows), :] = own_ref[...]
    for ref, side in ((first_ref, core), (second_ref, 1 - core)):
        at = (1 - shard) * rows + side * size
        for i in range(-(-width // BLOCK)):
            end = min((i + 1) * BLOCK, width)
            w_ref[pl.ds(at, size), i * BLOCK : end] = ref[(6 + i) * size : (7 + i) * size, : end - i * BLOCK]
    heads_ref[...] = jnp.concatenate([h0_ref[...], h1_ref[...], h2_ref[...]], axis=0)
    count = x_ref.shape[1]
    gain = gain_ref[:, 1:2]
    for at in range(0, count, BLOCK):
        cols = slice(at, at + BLOCK)
        m = x_ref[:, cols].astype(F32) + tn(w_ref[...], heads_ref[:, cols])
        r = lax.rsqrt(jnp.mean(m * m, axis=0, keepdims=True) + EPS)
        mid_ref[:, cols] = m
        n_ref[:, cols] = (m * r * gain).astype(BF)


def norm_back(x, gain, grad):
    r = lax.rsqrt(jnp.mean(x * x, axis=0, keepdims=True) + EPS)
    scaled = gain * grad
    dot = jnp.mean(scaled * x, axis=0, keepdims=True)
    return r * scaled - x * (r * r * r * dot)


def put(refs, ids_ref, half, shard, lane_half, rows, value):
    core = ids_ref[0]
    keep_ref, send_ref = refs
    s, y = flip(ids_ref[1], shard), flip(ids_ref[2], lane_half)
    one, two = jnp.where(core == 0, s, y), jnp.where(core == 0, y, s)

    @pl.when(core == half)
    def _():
        keep_ref[one, two, rows] = value

    @pl.when(core != half)
    def _():
        send_ref[two, one, rows] = value


def mlp_block(b, ids_ref, n_ref, cot_ref, wg_ref, wu_ref, wd_ref, first_ref, second_ref,
              acc_in, gn_in, refs, acc_ref, gn_ref, w, wd, act):
    core, shard = ids_ref[0], ids_ref[1]
    rows = wg_ref.shape[0]
    size = rows // 2
    hid = 2 * BLOCK
    blocks = wd_ref.shape[1] // BLOCK
    for i in range(4):
        part = slice(i * size, (i + 1) * size)
        own = (wg_ref, wu_ref)[i // 2][:, (i % 2 * blocks + b) * BLOCK : (i % 2 * blocks + b + 1) * BLOCK]
        fill(w.at[:, i * BLOCK : (i + 1) * BLOCK], core, shard, own, first_ref[part], second_ref[part], size)
    for s in range(2):
        cols = slice(s * BLOCK, (s + 1) * BLOCK)

        @pl.when(shard == s)
        def _():
            wd[:, cols] = wd_ref[:, b * BLOCK : (b + 1) * BLOCK]

        @pl.when(shard != s)
        def _():
            wd[pl.ds(core * rows, rows), cols] = first_ref[4 * size : 6 * size]
            wd[pl.ds((1 - core) * rows, rows), cols] = second_ref[4 * size : 6 * size]

    count = n_ref.shape[1]
    for at in range(0, count, BLOCK):
        cols = slice(at, at + BLOCK)
        both = tn(w[...], n_ref[:, cols])
        gate, up = both[:hid], both[hid:]
        gh = tn(wd[...], cot_ref[:, cols])
        sig = 0.5 * jnp.tanh(0.5 * gate) + 0.5
        a = gate * sig
        act[:hid, cols] = (a * up).astype(BF)
        act[hid : 2 * hid, cols] = (gh * up * (sig + a * (1.0 - sig))).astype(BF)
        act[2 * hid :, cols] = (gh * a).astype(BF)
        part = nn(wd[...], act[:hid, cols])
        gpart = nn(w[...], act[hid:, cols])
        acc_ref[:, cols] = part if acc_in is None else acc_in[:, cols] + part
        gn_ref[:, cols] = gpart if gn_in is None else gn_in[:, cols] + gpart
    for s in range(2):
        gd = nt(cot_ref[...], act[s * BLOCK : (s + 1) * BLOCK]).astype(BF)
        gg = nt(n_ref[...], act[hid + s * BLOCK : hid + (s + 1) * BLOCK]).astype(BF)
        gu = nt(n_ref[...], act[2 * hid + s * BLOCK : 2 * hid + (s + 1) * BLOCK]).astype(BF)
        for z in range(2):
            lanes = slice(z * LANES, (z + 1) * LANES)
            for half in range(2):
                part = slice(half * rows, (half + 1) * rows)
                put(refs, ids_ref, half, s, z, slice(0, rows), gd[part, lanes])
                put(refs, ids_ref, s, half, z, slice(rows, 2 * rows), gg[part, lanes])
                put(refs, ids_ref, s, half, z, slice(2 * rows, 3 * rows), gu[part, lanes])


def mlp_one_kernel(b, ids_ref, n_ref, cot_ref, wg, wu, wd, first, second, keep, send, acc, gn, *scratch):
    mlp_block(b, ids_ref, n_ref, cot_ref, wg, wu, wd, first, second, None, None, (keep, send), acc, gn, *scratch)


def mlp_two_kernel(b, ids_ref, n_ref, cot_ref, wg, wu, wd, first, second, acc_in, gn_in,
                   keep, send, acc, gn, *scratch):
    mlp_block(b, ids_ref, n_ref, cot_ref, wg, wu, wd, first, second, acc_in, gn_in, (keep, send), acc, gn, *scratch)


def between_kernel(ids_ref, cot_ref, acc, gn, mid_ref, gain_ref, heads_ref, wo_ref,
                   keep, send, out_ref, gmid_ref, gheads_ref):
    width, count = cot_ref.shape
    gain = gain_ref[:, 1:2]
    low = []
    for at in range(0, count, BLOCK):
        cols = slice(at, at + BLOCK)
        mid = mid_ref[:, cols]
        out_ref[:, cols] = (mid + acc[:, cols]).astype(BF)
        gm = cot_ref[:, cols].astype(F32) + norm_back(mid, gain, gn[:, cols])
        gmid_ref[:, cols] = gm
        low.append(gm.astype(BF))
        gheads_ref[:, cols] = nn(wo_ref[...], low[-1]).astype(BF)
    g = nt(heads_ref[...], jnp.concatenate(low, axis=1)).astype(BF)
    per = -(-(-(-width // LANES)) // 2)
    size = width // 4
    base = 0
    rest = keep.shape[2] - per * size
    for s in range(2):
        for half in range(2):
            rows = slice((2 * s + half) * size, (2 * s + half + 1) * size)
            for i in range(2 * per):
                end = min((i + 1) * LANES, width)
                value = g[rows, i * LANES : end] if end > i * LANES else None
                if value is None:
                    value = jnp.zeros((size, LANES), BF)
                elif end < (i + 1) * LANES:
                    value = jnp.concatenate([value, jnp.zeros((size, (i + 1) * LANES - end), BF)], axis=1)
                at = base + (i % per) * size
                put((keep, send), ids_ref, half, s, i // per, slice(at, at + size), value)
            if rest:
                for y in range(2):
                    put((keep, send), ids_ref, half, s, y, slice(base + per * size, base + per * size + rest),
                        jnp.zeros((rest, LANES), BF))


def attend_back_kernel(q_ref, k_ref, v_ref, o_ref, lse_ref, go_ref, cos_ref, sin_ref,
                       gq_ref, gk_ref, gv_ref, dk_ref, dv_ref):
    count = q_ref.shape[1]
    keys = k_ref[...].astype(F32).T.astype(BF)
    values = v_ref[...].astype(F32).T.astype(BF)
    dk_ref[...] = jnp.zeros_like(dk_ref)
    dv_ref[...] = jnp.zeros_like(dv_ref)
    for at in range(0, count, BLOCK):
        end = at + BLOCK
        cols = slice(at, end)
        q = beside(q_ref, cols)
        go = beside(go_ref, cols)
        delta = jnp.sum(go.astype(F32) * beside(o_ref, cols).astype(F32), axis=0, keepdims=True)
        lse = jnp.concatenate([lse_ref[h : h + 1, cols] for h in range(GROUP)], axis=1)
        s = causal(nn(keys[:end], q))
        p = jnp.exp(s - lse)
        ds = (p * (nn(values[:end], go) - delta)).astype(BF)
        dv_ref[:, :end] += nt(go, p.astype(BF))
        dk_ref[:, :end] += nt(q, ds)
        dq = nn(k_ref[:, :end], ds)
        c = cos_ref[:, cols] * 0.125
        sn = sin_ref[:, cols] * 0.125
        for h in range(GROUP):
            part = slice(h * BLOCK, (h + 1) * BLOCK)
            g1, g2 = dq[:HALF, part], dq[HALF:, part]
            row = h * HEAD_SIZE
            gq_ref[row : row + HALF, cols] = (g1 * c + g2 * sn).astype(BF)
            gq_ref[row + HALF : row + HEAD_SIZE, cols] = (g2 * c - g1 * sn).astype(BF)
    c = cos_ref[...]
    sn = sin_ref[...]
    g1, g2 = dk_ref[:HALF], dk_ref[HALF:]
    gk_ref[:HALF] = (g1 * c + g2 * sn).astype(BF)
    gk_ref[HALF:] = (g2 * c - g1 * sn).astype(BF)
    gv_ref[...] = dv_ref[...].astype(BF)


def weight_kernel(ids_ref, n_ref, *refs):
    count = (len(refs) - 2) // 3
    keep_ref, send_ref = refs[-2:]
    size, lanes = keep_ref.shape[2:]
    g = jnp.concatenate([refs[i * count + j][...] for i in range(3) for j in range(count)], axis=0)
    wide = g.shape[0]
    for z in range(2):
        end = min((z + 1) * lanes, wide)
        w = nt(n_ref[...], g[z * lanes : end]).astype(BF)
        if end < (z + 1) * lanes:
            w = jnp.concatenate([w, jnp.zeros((w.shape[0], (z + 1) * lanes - end), BF)], axis=1)
        for s in range(2):
            for half in range(2):
                at = (2 * s + half) * size
                put((keep_ref, send_ref), ids_ref, half, s, z, slice(0, size), w[at : at + size])


def tokens_kernel(x_ref, gain_ref, w_ref, gmid_ref, *refs):
    out_ref = refs[-1]
    parts = (len(refs) - 1) // 3
    count = x_ref.shape[1]
    gain = gain_ref[:, 0:1]
    for at in range(0, count, BLOCK):
        cols = slice(at, at + BLOCK)
        g = jnp.concatenate([refs[i * parts + j][:, cols] for i in range(3) for j in range(parts)], axis=0)
        gn = nn(w_ref[...], g)
        x = x_ref[:, cols].astype(F32)
        out_ref[:, cols] = (gmid_ref[:, cols] + norm_back(x, gain, gn)).astype(BF)


def plus(a, b):
    return (a.astype(F32) + b.astype(F32)).astype(BF)


def add_first_kernel(*refs):
    count = (len(refs) - 2) // 2
    send_ref, keep_ref = refs[-2:]
    at = 0
    for i in range(count):
        a, b = refs[i], refs[count + i]
        rows = slice(at, at + a.shape[2])
        at += a.shape[2]
        for j in range(2):
            send_ref[j, rows] = plus(a[1, j], b[1, j])
            keep_ref[j, rows] = plus(a[0, j], b[0, j])


def add_second_kernel(a_ref, b_ref, send_ref, keep_ref):
    send_ref[...] = plus(a_ref[1], b_ref[1])
    keep_ref[...] = plus(a_ref[0], b_ref[0])


def add_split_kernel(ids_ref, a_ref, b_ref, send_ref, keep_ref):
    z = ids_ref[3]
    rows = send_ref.shape[0]
    for ref, side in ((send_ref, 1 - z), (keep_ref, z)):
        part = pl.ds(side * rows, rows)
        ref[...] = plus(a_ref[part, :], b_ref[part, :])


def add_kernel(a_ref, b_ref, out_ref):
    out_ref[...] = plus(a_ref[...], b_ref[...])


def join_kernel(ids_ref, a_ref, b_ref, out_ref):
    z = ids_ref[3]
    rows = a_ref.shape[0]
    out_ref[pl.ds(z * rows, rows), :] = a_ref[...]
    out_ref[pl.ds((1 - z) * rows, rows), :] = b_ref[...]


def chosen(ids_ref, refs, half, y, rows):
    core, side = ids_ref[0], ids_ref[2]
    own, own_other, far, far_other = (ref[rows] for ref in refs)
    near = jnp.where(side == y, own, own_other)
    return jnp.where(core == half, near, jnp.where(side == y, far, far_other)).astype(F32)


def as_row(column_sums):
    rows = column_sums.shape[0]
    padded = -(-rows // LANES) * LANES
    if padded > rows:
        column_sums = jnp.concatenate([column_sums, jnp.zeros((padded - rows, LANES), F32)], axis=0)
    return jnp.sum(column_sums.T, axis=0, keepdims=True)[:, :rows]


def finish_first_kernel(ids_ref, a0, a1, a2, a3, wg_ref, wu_ref, gate_ref, up_ref, down_ref, total_ref):
    rows, ff = gate_ref.shape
    blocks = ff // 2 // BLOCK
    total = jnp.zeros((rows, LANES), F32)
    for b in range(blocks - 1):
        for z in range(2):
            for half in range(2):
                base = 3 * b * rows
                at = b * BLOCK + z * LANES
                down_ref[half * rows : (half + 1) * rows, at : at + LANES] = chosen(
                    ids_ref, (a0, a1, a2, a3), half, z, slice(base, base + rows))
                at += half * blocks * BLOCK
                for i, w_ref, to in ((1, wg_ref, gate_ref), (2, wu_ref, up_ref)):
                    g = chosen(ids_ref, (a0, a1, a2, a3), half, z, slice(base + i * rows, base + (i + 1) * rows))
                    to[:, at : at + LANES] = g
                    total += g * w_ref[:, at : at + LANES].astype(F32)
    total_ref[...] = total


def finish_last_kernel(ids_ref, b0, b1, b2, b3, wg_ref, wu_ref, total_in, gain_ref, gate_in, up_in, down_in,
                       gate_ref, up_ref, down_ref, out_ref, gain_out_ref, total_ref):
    half = pl.program_id(0)
    rows = gate_ref.shape[0]
    refs = (b0, b1, b2, b3)
    total = jnp.zeros((rows, LANES), F32)
    for z in range(2):
        lanes = slice(z * LANES, (z + 1) * LANES)
        down_ref[pl.ds(half * rows, rows), lanes] = chosen(ids_ref, refs, half, z, slice(0, rows))
        for i, w_ref, to in ((1, wg_ref, gate_ref), (2, wu_ref, up_ref)):
            g = chosen(ids_ref, refs, half, z, slice(i * rows, (i + 1) * rows))
            to[:, lanes] = g
            total += g * w_ref[:, lanes].astype(F32)

    @pl.when(half == 0)
    def _():
        total_ref[...] = total_in[...] + total

    @pl.when(half == 1)
    def _():
        gain_out_ref[...] = (as_row(total_ref[...] + total) / gain_ref[1:2, :rows])[0]
        width = out_ref.shape[1]
        pieces = -(-width // LANES)
        per = -(-pieces // 2)
        size = rows // 2
        for part in range(2):
            for i in range(pieces):
                end = min((i + 1) * LANES, width)
                at = 3 * rows + (i % per) * size
                g = chosen(ids_ref, refs, part, i // per, slice(at, at + size))
                out_ref[part * size : (part + 1) * size, i * LANES : end] = g[:, : end - i * LANES]


def finish_qkv_kernel(ids_ref, a0, a1, a2, a3, w_ref, gain_ref, q_ref, k_ref, v_ref, gain_out_ref, sum_ref):
    size, lanes = a0.shape
    wide_q, wide_k = q_ref.shape[1], k_ref.shape[1]
    wide = w_ref.shape[1]
    for half in range(2):
        rows = slice(half * size, (half + 1) * size)
        parts = [chosen(ids_ref, (a0, a1, a2, a3), half, z, slice(0, size)) for z in range(2)]
        g = jnp.concatenate(parts, axis=1)[:, :wide]
        q_ref[rows] = g[:, :wide_q]
        k_ref[rows] = g[:, wide_q : wide_q + wide_k]
        v_ref[rows] = g[:, wide_q + wide_k :]
        sums = jnp.sum(g * w_ref[rows].astype(F32), axis=1, keepdims=True)
        sum_ref[rows] = sums * (lax.broadcasted_iota(jnp.int32, (size, LANES), 1) == 0).astype(F32)
    gain_out_ref[...] = (as_row(sum_ref[...]) / gain_ref[0:1, : gain_out_ref.shape[0]])[0]


class Grid:
    def __init__(self, shards, replicas):
        self.shards, self.replicas = shards, replicas
        self.shard = lax.axis_index("shard")
        self.replica = lax.axis_index("replica")
        self.rest = [1 << i for i in range(3, replicas.bit_length() - 1)]
        self.ids = jnp.stack(
            [self.side(CORE), self.shard, self.side(SIDE), self.side(SPLIT)]
        ).astype(jnp.int32)

    def side(self, bit):
        return (self.replica // bit) % 2

    def swap(self, a, even, odd=None):
        odd = even if odd is None else odd
        pairs = []
        for s in range(self.shards):
            for r in range(self.replicas):
                shard, bit = odd if r % 2 else even
                pairs.append((s * self.replicas + r, (s ^ shard) * self.replicas + (r ^ bit)))
        return lax.ppermute(a, AXES, pairs)


def tie(values, others):
    return lax.optimization_barrier((tuple(values), tuple(others)))[0]


def flow(grid, keeps, sends, gots, split):
    rows = sum(k.shape[2] for k in keeps)
    lanes = keeps[0].shape[3]
    ops = 10**4
    after = yield sends
    gots = tie(gots, after)
    two = shape(2, rows, lanes)
    send, keep = call(add_first_kernel, "add_core", [two, two], ops,
                      in_specs=[whole()] * (2 * len(keeps)), out_specs=[whole()] * 2)(*keeps, *gots)
    got = grid.swap(send, (1, 0), (0, SIDE))
    after = yield [send]
    (got,) = tie([got], after)
    one = shape(rows, lanes)
    send, keep = call(add_second_kernel, "add_second", [one, one], ops,
                      in_specs=[whole()] * 2, out_specs=[whole()] * 2)(keep, got)
    got = grid.swap(send, (0, SIDE), (1, 0))
    after = yield [send]
    (got,) = tie([got], after)

    def add(a, b):
        return call(add_kernel, "add", shape(*a.shape), ops, in_specs=[whole()] * 2, out_specs=whole())(a, b)

    if split:
        half = shape(rows // 2, lanes)
        send, keep = call(add_split_kernel, "add_split", [half, half], ops,
                          in_specs=[smem()] + [whole()] * 2, out_specs=[whole()] * 2)(grid.ids, keep, got)
    else:
        send = keep = add(keep, got)
    got = grid.swap(send, (0, SPLIT))
    after = yield [send]
    (got,) = tie([got], after)
    a = add(keep, got)
    for bit in grid.rest[1:]:
        a = add(a, grid.swap(a, (0, bit)))
    got = grid.swap(a, (0, grid.rest[0]))
    after = yield [a]
    (got,) = tie([got], after)
    a = add(a, got)
    if split:
        got = grid.swap(a, (0, SPLIT))
        after = yield [a]
        (got,) = tie([got], after)
        a = call(join_kernel, "join", one, ops, in_specs=[smem()] + [whole()] * 2, out_specs=whole())(grid.ids, a, got)
    b = grid.swap(a, (0, SIDE))
    far = grid.swap(a, (0, CORE))
    after = yield [a]
    (b,) = tie([b], after)
    far_b = grid.swap(b, (0, CORE))
    yield a, b, far, far_b


def local(shards, replicas, tokens, cotangent, lengths, attn_gain, w_query, key_projection,
          value_projection, w_out, mlp_gain, w_gate, w_up, w_down):
    grid = Grid(shards, replicas)
    ids = grid.ids
    count, width = tokens.shape
    rows = w_query.shape[0]
    size = rows // 2
    ff = w_gate.shape[1]
    blocks = ff // 2 // BLOCK
    wide_k = key_projection.shape[1]
    wide = width + 2 * wide_k
    x = tokens.T
    cot = cotangent.T
    cos, sin = tables(count)
    own_down = w_down.T
    padded = -(-rows // LANES) * LANES
    other_one, other_two = grid.swap(attn_gain, (1, 0)), grid.swap(mlp_gain, (1, 0))
    none = jnp.zeros((6, rows), BF)
    gain_rows = jnp.concatenate([attn_gain[None], mlp_gain[None], none, other_one[None], other_two[None], none])
    gain_rows = jnp.pad(gain_rows.astype(F32), ((0, 0), (0, padded - rows)))

    own_qkv, half_qkv = call(
        pack_first_kernel, "pack_first", [shape(rows, wide), shape(size, wide)], 10**6, grid=(1,), limit=60,
        in_specs=[smem(), copied(rows, width), copied(rows, wide_k), copied(rows, wide_k)],
        out_specs=[copied(rows, wide), copied(size, wide)],
    )(ids, w_query, key_projection, value_projection)
    first_qkv = grid.swap(half_qkv, (1, 0))

    tall = [(6 + (-(-width // BLOCK) if b == 0 else 0)) * size for b in range(blocks)]
    (w_gate_,) = tie([w_gate], [half_qkv])
    pack_a, pack_b, pack_c = call(
        pack_kernel, "pack", [shape(t, BLOCK) for t in tall], 10**6, grid=(1,), limit=60,
        in_specs=[smem(), copied(rows, ff), copied(rows, ff), copied(width, ff // 2), copied(rows, width)],
        out_specs=[copied(t, BLOCK) for t in tall],
    )(ids, w_gate_, w_up, own_down, w_out)
    first_a = grid.swap(pack_a, (1, 0))
    (first_qkv,) = tie([first_qkv], [pack_a])
    second_qkv = grid.swap(first_qkv, (0, CORE))

    normed, q, k, v, w_qkv, gains = call(
        qkv_kernel, "qkv",
        [shape(width, count), shape(width, count), shape(wide_k, count), shape(wide_k, count), shape(width, wide),
         shape(width, 8, dtype=F32)],
        2 * count * width * wide, in_specs=[smem()] + [whole()] * 7, out_specs=[whole()] * 6,
    )(ids, x, gain_rows, own_qkv, first_qkv, second_qkv, cos, sin)
    first_b = grid.swap(tie([pack_b], [q])[0], (1, 0))

    group = GROUP * HEAD_SIZE

    def of_group(g):
        block_q = pl.BlockSpec((group, count), lambda i: (g, 0))
        return block_q, pl.BlockSpec((HEAD_SIZE, count), lambda i: (g, 0))

    heads, lse = [], []
    q_ = q
    for g in range(KEY_VALUE_HEADS):
        block_q, block_k = of_group(g)
        o, l = call(
            attend_kernel, "attend", [shape(group, count), shape(8, count, dtype=F32)], 8 * count * count * group,
            grid=(1,), in_specs=[block_q, block_k, block_k], out_specs=[copied(group, count), copied(8, count)], limit=20,
        )(q_, k, v)
        heads.append(o)
        lse.append(l)
        (q_,) = tie([q], [o])
    first_c = grid.swap(tie([pack_c], heads[:1])[0], (1, 0))
    (first_a,) = tie([first_a], heads)
    second_a = grid.swap(first_a, (0, CORE))

    middle, normed_two, w_o, all_heads = call(
        middle_kernel, "middle",
        [shape(width, count, dtype=F32), shape(width, count), shape(width, width), shape(width, count)],
        2 * count * width * width, in_specs=[smem()] + [whole()] * 8, out_specs=[whole()] * 4,
    )(ids, x, *heads, w_out, first_a, second_a, gains)

    scratch = [pltpu.VMEM((width, 4 * BLOCK), BF), pltpu.VMEM((width, 2 * BLOCK), BF), pltpu.VMEM((6 * BLOCK, count), BF)]
    float_act = shape(width, count, dtype=F32)

    def mlp(kernel, b, outs, first, second, more):
        return call(
            functools.partial(kernel, b), "mlp", outs, 18 * count * width * ff // blocks,
            in_specs=[smem()] + [whole()] * (7 + len(more)), out_specs=[whole()] * len(outs),
            scratch=scratch, limit=24, weight=10,
        )(ids, normed_two, cot, w_gate, w_up, own_down, first, second, *more)

    part = (2, 2, 3 * rows, LANES)
    keep_a, send_a, acc, gn = mlp(mlp_one_kernel, 0, [shape(*part)] * 2 + [float_act] * 2, first_a, second_a, [])
    (first_b,) = tie([first_b], [acc])
    second_b = grid.swap(first_b, (0, CORE))
    got_a = grid.swap(send_a, (0, CORE))
    keep_b, send_b, acc, gn = mlp(
        mlp_two_kernel, 1, [shape(*part)] * 2 + [float_act] * 2, first_b, second_b, [acc, gn])
    got_b = grid.swap(send_b, (0, CORE))
    (first_c,) = tie([first_c], [acc])
    second_c = grid.swap(first_c, (0, CORE))
    keep_c, send_c, acc, gn = mlp(
        mlp_two_kernel, 2, [shape(*part)] * 2 + [float_act] * 2, first_c, second_c, [acc, gn])
    got_c = grid.swap(send_c, (0, CORE))
    flows = {"a": flow(grid, [keep_a, keep_b], [send_a, send_b], [got_a, got_b], True)}
    next(flows["a"])
    sums = {}
    state = {"after": [acc]}

    def step(names):
        for name in names:
            sent = flows[name].send(state["after"])
            if len(sent) == 4:
                sums[name] = sent
            else:
                state["after"] = sent

    def then(value):
        return tie([value], state["after"])[0]

    step("a")
    per = -(-(-(-width // LANES)) // 2)
    part_o = (2, 2, -(-per * size // 32) * 32, LANES)
    keep_o, send_o, out, g_mid, g_heads = call(
        between_kernel, "between",
        [shape(*part_o), shape(*part_o), shape(width, count), float_act, shape(width, count)],
        4 * count * width * width, in_specs=[smem()] + [whole()] * 7, out_specs=[whole()] * 5, limit=24, weight=10,
    )(ids, then(cot), acc, gn, middle, gains, all_heads, w_o)
    flows["b"] = flow(grid, [keep_c, keep_o], [send_c, send_o], [got_c, grid.swap(send_o, (0, CORE))], True)
    next(flows["b"])
    state["after"] = [g_heads]

    grads = []
    for g, name in enumerate(('ba', '', 'ba')):
        block_q, block_k = of_group(g)
        out_q, out_k = copied(group, count), copied(HEAD_SIZE, count)
        grads.append(call(
            attend_back_kernel, "attend_back", [shape(group, count), shape(HEAD_SIZE, count), shape(HEAD_SIZE, count)],
            4 * count * count * width, grid=(1,),
            in_specs=[block_q, block_k, block_k, out_q, copied(8, count), block_q] + [copied(HALF, count)] * 2,
            out_specs=[out_q, out_k, out_k],
            scratch=[pltpu.VMEM((HEAD_SIZE, count), F32)] * 2, limit=24, weight=10 if g == 0 else 1,
        )(q, k, v, heads[g], lse[g], then(g_heads), cos, sin))
        state["after"] = [grads[-1][2]]
        step(name)
    grads = [g[i] for i in range(3) for g in grads]

    lanes = -(-wide // (2 * LANES)) * LANES
    part_three = (2, 2, size, lanes)
    keep_d, send_d = call(
        weight_kernel, "weights", [shape(*part_three), shape(*part_three)], 2 * count * width * wide,
        in_specs=[smem()] + [whole()] * 10, out_specs=[whole()] * 2,
    )(ids, then(normed), *grads)
    flows["d"] = flow(grid, [keep_d], [send_d], [grid.swap(send_d, (0, CORE))], False)
    next(flows["d"])
    state["after"] = [send_d]
    step("dab")
    grad_tokens = call(
        tokens_kernel, "grad_tokens", shape(width, count), 2 * count * width * wide,
        in_specs=[whole()] * 13, out_specs=whole(),
    )(then(x), gains, w_qkv, g_mid, *grads)
    state["after"] = [grad_tokens]
    step("dbdadbadbad")
    g_gate, g_up, g_down, partial = call(
        finish_first_kernel, "finish_first",
        [shape(rows, ff, dtype=F32), shape(rows, ff, dtype=F32), shape(width, ff // 2, dtype=F32),
         shape(rows, LANES, dtype=F32)],
        10**7, in_specs=[smem()] + [whole()] * 6, out_specs=[whole()] * 4,
    )(ids, *sums["a"], then(w_gate), w_up)
    g_query, g_key, g_value, g_gain_one = call(
        finish_qkv_kernel, "finish_qkv",
        [shape(rows, width, dtype=F32), shape(rows, wide_k, dtype=F32), shape(rows, wide_k, dtype=F32),
         shape(rows, dtype=F32)],
        10**7, in_specs=[smem()] + [whole()] * 6, out_specs=[whole()] * 4, scratch=[pltpu.VMEM((rows, LANES), F32)],
    )(ids, *sums["d"], tie([own_qkv], [partial])[0], gain_rows)
    state["after"] = [partial]
    step("b")
    piece = pl.BlockSpec((rows, BLOCK), lambda i: (0, (i + 1) * blocks - 1))
    last = pl.BlockSpec((width, BLOCK), lambda i: (0, blocks - 1))
    kept = pl.BlockSpec(memory_space=pl.ANY)
    tall = sums["b"][0].shape
    g_gate, g_up, g_down, g_out, g_gain_two = call(
        finish_last_kernel, "finish_last",
        [shape(rows, ff, dtype=F32), shape(rows, ff, dtype=F32), shape(width, ff // 2, dtype=F32),
         shape(rows, width, dtype=F32), shape(rows, dtype=F32)],
        10**7, grid=(2,),
        in_specs=[smem()] + [copied(*tall)] * 4 + [piece, piece, copied(rows, LANES), copied(16, padded)] + [kept] * 3,
        out_specs=[piece, piece, last, copied(rows, width), copied(rows)],
        scratch=[pltpu.VMEM((rows, LANES), F32)], aliases={9: 0, 10: 1, 11: 2},
    )(ids, *sums["b"], w_gate, w_up, partial, gain_rows, g_gate, g_up, g_down)
    return (
        out.T,
        grad_tokens.T,
        g_gain_one,
        g_query,
        g_key,
        g_value,
        g_out,
        g_gain_two,
        g_gate,
        g_up,
        g_down.T,
    )


def solution(mesh):
    tokens = P(AXES, None)
    split = P("shard", None)
    gain = P("shard")
    return jax.shard_map(
        functools.partial(local, mesh.shape["shard"], mesh.shape["replica"]),
        mesh=mesh,
        in_specs=(tokens, tokens, tokens, gain, split, split, split, split, gain, split, split, split),
        out_specs=(tokens, tokens, gain, split, split, split, split, gain, split, split, split),
        check_vma=False,
    )
```

```python
import functools
import math

import jax
import jax.numpy as jnp
import numpy as np
from jax import lax
from jax.experimental import pallas as pl
from jax.experimental.pallas import tpu as pltpu
from jax.sharding import PartitionSpec as P

QUERY_HEADS = 9
KEY_VALUE_HEADS = 3
HEAD_SIZE = 64
HALF = HEAD_SIZE // 2
GROUP = QUERY_HEADS // KEY_VALUE_HEADS
EPS = 1e-05
THETA = 100000.0
BF = jnp.bfloat16
F32 = jnp.float32
BLOCK = 256
AXES = ("shard", "replica")
LANES = 128
TIMES = dict(pack_first=2, pack=3, qkv=3.6, attend=3, middle=2.2, mlp=9, between=5.5, attend_back=5, weights=2.4,
             grad_tokens=3.5, finish_first=3.7, finish_qkv=2, finish_last=2.6, add_core=0.4, add_second=0.4,
             add_split=0.5, add=0.3, join=0.6, pause=10)
CORE, SIDE, SPLIT = 1, 2, 4


def nn(a, b):
    return lax.dot_general(a, b, (((1,), (0,)), ((), ())), preferred_element_type=F32)


def nt(a, b):
    return lax.dot_general(a, b, (((1,), (1,)), ((), ())), preferred_element_type=F32)


def tn(a, b):
    return lax.dot_general(a, b, (((0,), (0,)), ((), ())), preferred_element_type=F32)


def whole():
    return pl.BlockSpec(memory_space=pltpu.VMEM)


def call(kernel, name, outs, flops, grid=None, in_specs=None, out_specs=None, scratch=(), limit=16, weight=1, aliases=None):
    return pl.pallas_call(
        kernel,
        name=name,
        out_shape=outs,
        grid=grid or (),
        in_specs=in_specs,
        out_specs=out_specs,
        scratch_shapes=list(scratch),
        compiler_params=pltpu.CompilerParams(vmem_limit_bytes=limit * 2**20),
        input_output_aliases=aliases or {},
        cost_estimate=pl.CostEstimate(flops=int(TIMES[name] * 0.46 * 10**9), bytes_accessed=1024, transcendentals=0),
    )


def copied(*dims):
    return pl.BlockSpec(dims, lambda i: (0,) * len(dims))


def shape(*dims, dtype=BF):
    return jax.ShapeDtypeStruct(dims, dtype)


def tables(count):
    inverse = np.exp(np.arange(HALF, dtype=np.float32) * np.float32(-2.0 * math.log(THETA) / HEAD_SIZE))
    angles = jnp.arange(count, dtype=jnp.int32).astype(F32)[None, :] * jnp.asarray(inverse)[:, None]
    return jnp.cos(angles), jnp.sin(angles)

def smem():
    return pl.BlockSpec(memory_space=pltpu.SMEM)


def flip(a, b):
    return lax.rem(a + b, 2)


def pack_first_kernel(ids_ref, wq_ref, wk_ref, wv_ref, own_ref, half_ref):
    size = half_ref.shape[0]
    own_ref[...] = jnp.concatenate([wq_ref[...], wk_ref[...], wv_ref[...]], axis=1)
    half_ref[...] = own_ref[pl.ds(ids_ref[0] * size, size), :]


def pack_kernel(ids_ref, wg_ref, wu_ref, wd_ref, wo_ref, *out_refs):
    core = ids_ref[0]
    rows, width = wo_ref.shape
    size = rows // 2
    mine = pl.ds(core * size, size)
    blocks = len(out_refs)
    for b, out_ref in enumerate(out_refs):
        for s in range(2):
            cols = slice((s * blocks + b) * BLOCK, (s * blocks + b + 1) * BLOCK)
            out_ref[s * size : (s + 1) * size, :] = wg_ref[mine, cols]
            out_ref[(2 + s) * size : (3 + s) * size, :] = wu_ref[mine, cols]
        out_ref[4 * size : 6 * size, :] = wd_ref[pl.ds(core * rows, rows), b * BLOCK : (b + 1) * BLOCK]
    for i in range(-(-width // BLOCK)):
        end = min((i + 1) * BLOCK, width)
        piece = wo_ref[mine, i * BLOCK : end]
        if end < (i + 1) * BLOCK:
            piece = jnp.concatenate([piece, jnp.zeros((size, (i + 1) * BLOCK - end), BF)], axis=1)
        out_refs[0][(6 + i) * size : (7 + i) * size, :] = piece


def fill(to, core, shard, own, first, second, size):
    rows = 2 * size
    to[pl.ds(shard * rows, rows), :] = own
    to[pl.ds((1 - shard) * rows + core * size, size), :] = first
    to[pl.ds((1 - shard) * rows + (1 - core) * size, size), :] = second


def qkv_kernel(ids_ref, x_ref, gain_ref, own_ref, first_ref, second_ref, cos_ref, sin_ref,
               n_ref, q_ref, k_ref, v_ref, w_ref, gains_ref):
    core, shard = ids_ref[0], ids_ref[1]
    rows = own_ref.shape[0]
    size = rows // 2
    fill(w_ref, core, shard, own_ref[...], first_ref[...], second_ref[...], size)
    columns = gain_ref[...].T[:rows]
    gains_ref[pl.ds(shard * rows, rows), :] = columns[:, 0:8]
    gains_ref[pl.ds((1 - shard) * rows, rows), :] = columns[:, 8:16]
    count = x_ref.shape[1]
    gain = gains_ref[:, 0:1]
    width_q = q_ref.shape[0]
    width_k = k_ref.shape[0]
    for at in range(0, count, BLOCK):
        cols = slice(at, at + BLOCK)
        x = x_ref[:, cols].astype(F32)
        r = lax.rsqrt(jnp.mean(x * x, axis=0, keepdims=True) + EPS)
        n = (x * r * gain).astype(BF)
        n_ref[:, cols] = n
        y = tn(w_ref[...], n)
        c = cos_ref[:, cols]
        s = sin_ref[:, cols]
        cq, sq = c * 0.125, s * 0.125
        for head in range((width_q + width_k) // HEAD_SIZE):
            row = head * HEAD_SIZE
            u1 = y[row : row + HALF]
            u2 = y[row + HALF : row + HEAD_SIZE]
            if row < width_q:
                q_ref[row : row + HALF, cols] = (u1 * cq - u2 * sq).astype(BF)
                q_ref[row + HALF : row + HEAD_SIZE, cols] = (u2 * cq + u1 * sq).astype(BF)
            else:
                row -= width_q
                k_ref[row : row + HALF, cols] = (u1 * c - u2 * s).astype(BF)
                k_ref[row + HALF : row + HEAD_SIZE, cols] = (u2 * c + u1 * s).astype(BF)
        v_ref[:, cols] = y[width_q + width_k :].astype(BF)


def causal(s):
    low = s.shape[0] - BLOCK
    rows = lax.broadcasted_iota(jnp.int32, (BLOCK, BLOCK), 0)
    cols = lax.broadcasted_iota(jnp.int32, (BLOCK, BLOCK), 1)
    keep = jnp.concatenate([rows <= cols] * (s.shape[1] // BLOCK), axis=1)
    last = jnp.where(keep, s[low:], -1e30)
    return last if low == 0 else jnp.concatenate([s[:low], last], axis=0)


def beside(ref, cols):
    return jnp.concatenate(
        [ref[h * HEAD_SIZE : (h + 1) * HEAD_SIZE, cols] for h in range(GROUP)], axis=1
    )


def attend_kernel(q_ref, k_ref, v_ref, o_ref, lse_ref):
    count = q_ref.shape[1]
    keys = k_ref[...].astype(F32).T.astype(BF)
    for at in range(0, count, BLOCK):
        end = at + BLOCK
        cols = slice(at, end)
        s = causal(nn(keys[:end], beside(q_ref, cols)))
        top = jnp.max(s, axis=0, keepdims=True)
        p = jnp.exp(s - top)
        total = jnp.sum(p, axis=0, keepdims=True)
        o = nn(v_ref[:, :end], p.astype(BF)) / total
        lse = top + jnp.log(total)
        for h in range(GROUP):
            part = slice(h * BLOCK, (h + 1) * BLOCK)
            o_ref[h * HEAD_SIZE : (h + 1) * HEAD_SIZE, cols] = o[:, part].astype(BF)
            lse_ref[h : h + 1, cols] = lse[:, part]


def middle_kernel(ids_ref, x_ref, h0_ref, h1_ref, h2_ref, own_ref, first_ref, second_ref, gain_ref, mid_ref, n_ref, w_ref, heads_ref):
    core, shard = ids_ref[0], ids_ref[1]
    rows, width = own_ref.shape
    size = rows // 2
    w_ref[pl.ds(shard * rows, rows), :] = own_ref[...]
    for ref, side in ((first_ref, core), (second_ref, 1 - core)):
        at = (1 - shard) * rows + side * size
        for i in range(-(-width // BLOCK)):
            end = min((i + 1) * BLOCK, width)
            w_ref[pl.ds(at, size), i * BLOCK : end] = ref[(6 + i) * size : (7 + i) * size, : end - i * BLOCK]
    heads_ref[...] = jnp.concatenate([h0_ref[...], h1_ref[...], h2_ref[...]], axis=0)
    count = x_ref.shape[1]
    gain = gain_ref[:, 1:2]
    for at in range(0, count, BLOCK):
        cols = slice(at, at + BLOCK)
        m = x_ref[:, cols].astype(F32) + tn(w_ref[...], heads_ref[:, cols])
        r = lax.rsqrt(jnp.mean(m * m, axis=0, keepdims=True) + EPS)
        mid_ref[:, cols] = m
        n_ref[:, cols] = (m * r * gain).astype(BF)


def norm_back(x, gain, grad):
    r = lax.rsqrt(jnp.mean(x * x, axis=0, keepdims=True) + EPS)
    scaled = gain * grad
    dot = jnp.mean(scaled * x, axis=0, keepdims=True)
    return r * scaled - x * (r * r * r * dot)


def put(refs, ids_ref, half, shard, lane_half, rows, value):
    core = ids_ref[0]
    keep_ref, send_ref = refs
    s, y = flip(ids_ref[1], shard), flip(ids_ref[2], lane_half)
    one, two = jnp.where(core == 0, s, y), jnp.where(core == 0, y, s)

    @pl.when(core == half)
    def _():
        keep_ref[one, two, rows] = value

    @pl.when(core != half)
    def _():
        send_ref[two, one, rows] = value


def mlp_block(b, ids_ref, n_ref, cot_ref, wg_ref, wu_ref, wd_ref, first_ref, second_ref,
              acc_in, gn_in, refs, acc_ref, gn_ref, w, wd, act):
    core, shard = ids_ref[0], ids_ref[1]
    rows = wg_ref.shape[0]
    size = rows // 2
    hid = 2 * BLOCK
    blocks = wd_ref.shape[1] // BLOCK
    for i in range(4):
        part = slice(i * size, (i + 1) * size)
        own = (wg_ref, wu_ref)[i // 2][:, (i % 2 * blocks + b) * BLOCK : (i % 2 * blocks + b + 1) * BLOCK]
        fill(w.at[:, i * BLOCK : (i + 1) * BLOCK], core, shard, own, first_ref[part], second_ref[part], size)
    for s in range(2):
        cols = slice(s * BLOCK, (s + 1) * BLOCK)

        @pl.when(shard == s)
        def _():
            wd[:, cols] = wd_ref[:, b * BLOCK : (b + 1) * BLOCK]

        @pl.when(shard != s)
        def _():
            wd[pl.ds(core * rows, rows), cols] = first_ref[4 * size : 6 * size]
            wd[pl.ds((1 - core) * rows, rows), cols] = second_ref[4 * size : 6 * size]

    count = n_ref.shape[1]
    for at in range(0, count, BLOCK):
        cols = slice(at, at + BLOCK)
        both = tn(w[...], n_ref[:, cols])
        gate, up = both[:hid], both[hid:]
        gh = tn(wd[...], cot_ref[:, cols])
        sig = 0.5 * jnp.tanh(0.5 * gate) + 0.5
        a = gate * sig
        act[:hid, cols] = (a * up).astype(BF)
        act[hid : 2 * hid, cols] = (gh * up * (sig + a * (1.0 - sig))).astype(BF)
        act[2 * hid :, cols] = (gh * a).astype(BF)
        part = nn(wd[...], act[:hid, cols])
        gpart = nn(w[...], act[hid:, cols])
        acc_ref[:, cols] = part if acc_in is None else acc_in[:, cols] + part
        gn_ref[:, cols] = gpart if gn_in is None else gn_in[:, cols] + gpart
    for s in range(2):
        gd = nt(cot_ref[...], act[s * BLOCK : (s + 1) * BLOCK]).astype(BF)
        gg = nt(n_ref[...], act[hid + s * BLOCK : hid + (s + 1) * BLOCK]).astype(BF)
        gu = nt(n_ref[...], act[2 * hid + s * BLOCK : 2 * hid + (s + 1) * BLOCK]).astype(BF)
        for z in range(2):
            lanes = slice(z * LANES, (z + 1) * LANES)
            for half in range(2):
                part = slice(half * rows, (half + 1) * rows)
                put(refs, ids_ref, half, s, z, slice(0, rows), gd[part, lanes])
                put(refs, ids_ref, s, half, z, slice(rows, 2 * rows), gg[part, lanes])
                put(refs, ids_ref, s, half, z, slice(2 * rows, 3 * rows), gu[part, lanes])


def mlp_one_kernel(b, ids_ref, n_ref, cot_ref, wg, wu, wd, first, second, keep, send, acc, gn, *scratch):
    mlp_block(b, ids_ref, n_ref, cot_ref, wg, wu, wd, first, second, None, None, (keep, send), acc, gn, *scratch)


def mlp_two_kernel(b, ids_ref, n_ref, cot_ref, wg, wu, wd, first, second, acc_in, gn_in,
                   keep, send, acc, gn, *scratch):
    mlp_block(b, ids_ref, n_ref, cot_ref, wg, wu, wd, first, second, acc_in, gn_in, (keep, send), acc, gn, *scratch)


def between_kernel(ids_ref, cot_ref, acc, gn, mid_ref, gain_ref, heads_ref, wo_ref,
                   keep, send, out_ref, gmid_ref, gheads_ref):
    width, count = cot_ref.shape
    gain = gain_ref[:, 1:2]
    low = []
    for at in range(0, count, BLOCK):
        cols = slice(at, at + BLOCK)
        mid = mid_ref[:, cols]
        out_ref[:, cols] = (mid + acc[:, cols]).astype(BF)
        gm = cot_ref[:, cols].astype(F32) + norm_back(mid, gain, gn[:, cols])
        gmid_ref[:, cols] = gm
        low.append(gm.astype(BF))
        gheads_ref[:, cols] = nn(wo_ref[...], low[-1]).astype(BF)
    g = nt(heads_ref[...], jnp.concatenate(low, axis=1)).astype(BF)
    per = -(-(-(-width // LANES)) // 2)
    size = width // 4
    base = 0
    rest = keep.shape[2] - per * size
    for s in range(2):
        for half in range(2):
            rows = slice((2 * s + half) * size, (2 * s + half + 1) * size)
            for i in range(2 * per):
                end = min((i + 1) * LANES, width)
                value = g[rows, i * LANES : end] if end > i * LANES else None
                if value is None:
                    value = jnp.zeros((size, LANES), BF)
                elif end < (i + 1) * LANES:
                    value = jnp.concatenate([value, jnp.zeros((size, (i + 1) * LANES - end), BF)], axis=1)
                at = base + (i % per) * size
                put((keep, send), ids_ref, half, s, i // per, slice(at, at + size), value)
            if rest:
                for y in range(2):
                    put((keep, send), ids_ref, half, s, y, slice(base + per * size, base + per * size + rest),
                        jnp.zeros((rest, LANES), BF))


def attend_back_kernel(q_ref, k_ref, v_ref, o_ref, lse_ref, go_ref, cos_ref, sin_ref,
                       gq_ref, gk_ref, gv_ref, dk_ref, dv_ref):
    count = q_ref.shape[1]
    keys = k_ref[...].astype(F32).T.astype(BF)
    values = v_ref[...].astype(F32).T.astype(BF)
    dk_ref[...] = jnp.zeros_like(dk_ref)
    dv_ref[...] = jnp.zeros_like(dv_ref)
    for at in range(0, count, BLOCK):
        end = at + BLOCK
        cols = slice(at, end)
        q = beside(q_ref, cols)
        go = beside(go_ref, cols)
        delta = jnp.sum(go.astype(F32) * beside(o_ref, cols).astype(F32), axis=0, keepdims=True)
        lse = jnp.concatenate([lse_ref[h : h + 1, cols] for h in range(GROUP)], axis=1)
        s = causal(nn(keys[:end], q))
        p = jnp.exp(s - lse)
        ds = (p * (nn(values[:end], go) - delta)).astype(BF)
        dv_ref[:, :end] += nt(go, p.astype(BF))
        dk_ref[:, :end] += nt(q, ds)
        dq = nn(k_ref[:, :end], ds)
        c = cos_ref[:, cols] * 0.125
        sn = sin_ref[:, cols] * 0.125
        for h in range(GROUP):
            part = slice(h * BLOCK, (h + 1) * BLOCK)
            g1, g2 = dq[:HALF, part], dq[HALF:, part]
            row = h * HEAD_SIZE
            gq_ref[row : row + HALF, cols] = (g1 * c + g2 * sn).astype(BF)
            gq_ref[row + HALF : row + HEAD_SIZE, cols] = (g2 * c - g1 * sn).astype(BF)
    c = cos_ref[...]
    sn = sin_ref[...]
    g1, g2 = dk_ref[:HALF], dk_ref[HALF:]
    gk_ref[:HALF] = (g1 * c + g2 * sn).astype(BF)
    gk_ref[HALF:] = (g2 * c - g1 * sn).astype(BF)
    gv_ref[...] = dv_ref[...].astype(BF)


def weight_kernel(ids_ref, n_ref, *refs):
    count = (len(refs) - 2) // 3
    keep_ref, send_ref = refs[-2:]
    size, lanes = keep_ref.shape[2:]
    g = jnp.concatenate([refs[i * count + j][...] for i in range(3) for j in range(count)], axis=0)
    wide = g.shape[0]
    for z in range(2):
        end = min((z + 1) * lanes, wide)
        w = nt(n_ref[...], g[z * lanes : end]).astype(BF)
        if end < (z + 1) * lanes:
            w = jnp.concatenate([w, jnp.zeros((w.shape[0], (z + 1) * lanes - end), BF)], axis=1)
        for s in range(2):
            for half in range(2):
                at = (2 * s + half) * size
                put((keep_ref, send_ref), ids_ref, half, s, z, slice(0, size), w[at : at + size])


def tokens_kernel(x_ref, gain_ref, w_ref, gmid_ref, *refs):
    out_ref = refs[-1]
    parts = (len(refs) - 1) // 3
    count = x_ref.shape[1]
    gain = gain_ref[:, 0:1]
    for at in range(0, count, BLOCK):
        cols = slice(at, at + BLOCK)
        g = jnp.concatenate([refs[i * parts + j][:, cols] for i in range(3) for j in range(parts)], axis=0)
        gn = nn(w_ref[...], g)
        x = x_ref[:, cols].astype(F32)
        out_ref[:, cols] = (gmid_ref[:, cols] + norm_back(x, gain, gn)).astype(BF)


def plus(a, b):
    return (a.astype(F32) + b.astype(F32)).astype(BF)


def add_first_kernel(*refs):
    count = (len(refs) - 2) // 2
    send_ref, keep_ref = refs[-2:]
    at = 0
    for i in range(count):
        a, b = refs[i], refs[count + i]
        rows = slice(at, at + a.shape[2])
        at += a.shape[2]
        for j in range(2):
            send_ref[j, rows] = plus(a[1, j], b[1, j])
            keep_ref[j, rows] = plus(a[0, j], b[0, j])


def add_second_kernel(a_ref, b_ref, send_ref, keep_ref):
    send_ref[...] = plus(a_ref[1], b_ref[1])
    keep_ref[...] = plus(a_ref[0], b_ref[0])


def add_split_kernel(ids_ref, a_ref, b_ref, send_ref, keep_ref):
    z = ids_ref[3]
    rows = send_ref.shape[0]
    for ref, side in ((send_ref, 1 - z), (keep_ref, z)):
        part = pl.ds(side * rows, rows)
        ref[...] = plus(a_ref[part, :], b_ref[part, :])


def add_kernel(a_ref, b_ref, out_ref):
    out_ref[...] = plus(a_ref[...], b_ref[...])


def join_kernel(ids_ref, a_ref, b_ref, out_ref):
    z = ids_ref[3]
    rows = a_ref.shape[0]
    out_ref[pl.ds(z * rows, rows), :] = a_ref[...]
    out_ref[pl.ds((1 - z) * rows, rows), :] = b_ref[...]


def chosen(ids_ref, refs, half, y, rows):
    core, side = ids_ref[0], ids_ref[2]
    own, own_other, far, far_other = (ref[rows] for ref in refs)
    near = jnp.where(side == y, own, own_other)
    return jnp.where(core == half, near, jnp.where(side == y, far, far_other)).astype(F32)


def as_row(column_sums):
    rows = column_sums.shape[0]
    padded = -(-rows // LANES) * LANES
    if padded > rows:
        column_sums = jnp.concatenate([column_sums, jnp.zeros((padded - rows, LANES), F32)], axis=0)
    return jnp.sum(column_sums.T, axis=0, keepdims=True)[:, :rows]


def finish_first_kernel(ids_ref, a0, a1, a2, a3, wg_ref, wu_ref, gate_ref, up_ref, down_ref, total_ref):
    rows, ff = gate_ref.shape
    blocks = ff // 2 // BLOCK
    total = jnp.zeros((rows, LANES), F32)
    for b in range(blocks - 1):
        for z in range(2):
            for half in range(2):
                base = 3 * b * rows
                at = b * BLOCK + z * LANES
                down_ref[half * rows : (half + 1) * rows, at : at + LANES] = chosen(
                    ids_ref, (a0, a1, a2, a3), half, z, slice(base, base + rows))
                at += half * blocks * BLOCK
                for i, w_ref, to in ((1, wg_ref, gate_ref), (2, wu_ref, up_ref)):
                    g = chosen(ids_ref, (a0, a1, a2, a3), half, z, slice(base + i * rows, base + (i + 1) * rows))
                    to[:, at : at + LANES] = g
                    total += g * w_ref[:, at : at + LANES].astype(F32)
    total_ref[...] = total


def finish_last_kernel(ids_ref, b0, b1, b2, b3, wg_ref, wu_ref, total_in, gain_ref, gate_in, up_in, down_in,
                       gate_ref, up_ref, down_ref, out_ref, gain_out_ref, total_ref):
    half = pl.program_id(0)
    rows = gate_ref.shape[0]
    refs = (b0, b1, b2, b3)
    total = jnp.zeros((rows, LANES), F32)
    for z in range(2):
        lanes = slice(z * LANES, (z + 1) * LANES)
        down_ref[pl.ds(half * rows, rows), lanes] = chosen(ids_ref, refs, half, z, slice(0, rows))
        for i, w_ref, to in ((1, wg_ref, gate_ref), (2, wu_ref, up_ref)):
            g = chosen(ids_ref, refs, half, z, slice(i * rows, (i + 1) * rows))
            to[:, lanes] = g
            total += g * w_ref[:, lanes].astype(F32)

    @pl.when(half == 0)
    def _():
        total_ref[...] = total_in[...] + total

    @pl.when(half == 1)
    def _():
        gain_out_ref[...] = (as_row(total_ref[...] + total) / gain_ref[1:2, :rows])[0]
        width = out_ref.shape[1]
        pieces = -(-width // LANES)
        per = -(-pieces // 2)
        size = rows // 2
        for part in range(2):
            for i in range(pieces):
                end = min((i + 1) * LANES, width)
                at = 3 * rows + (i % per) * size
                g = chosen(ids_ref, refs, part, i // per, slice(at, at + size))
                out_ref[part * size : (part + 1) * size, i * LANES : end] = g[:, : end - i * LANES]


def finish_qkv_kernel(ids_ref, a0, a1, a2, a3, w_ref, gain_ref, q_ref, k_ref, v_ref, gain_out_ref, sum_ref):
    size, lanes = a0.shape
    wide_q, wide_k = q_ref.shape[1], k_ref.shape[1]
    wide = w_ref.shape[1]
    for half in range(2):
        rows = slice(half * size, (half + 1) * size)
        parts = [chosen(ids_ref, (a0, a1, a2, a3), half, z, slice(0, size)) for z in range(2)]
        g = jnp.concatenate(parts, axis=1)[:, :wide]
        q_ref[rows] = g[:, :wide_q]
        k_ref[rows] = g[:, wide_q : wide_q + wide_k]
        v_ref[rows] = g[:, wide_q + wide_k :]
        sums = jnp.sum(g * w_ref[rows].astype(F32), axis=1, keepdims=True)
        sum_ref[rows] = sums * (lax.broadcasted_iota(jnp.int32, (size, LANES), 1) == 0).astype(F32)
    gain_out_ref[...] = (as_row(sum_ref[...]) / gain_ref[0:1, : gain_out_ref.shape[0]])[0]


class Grid:
    def __init__(self, shards, replicas):
        self.shards, self.replicas = shards, replicas
        self.shard = lax.axis_index("shard")
        self.replica = lax.axis_index("replica")
        self.rest = [1 << i for i in range(3, replicas.bit_length() - 1)]
        self.ids = jnp.stack(
            [self.side(CORE), self.shard, self.side(SIDE), self.side(SPLIT)]
        ).astype(jnp.int32)

    def side(self, bit):
        return (self.replica // bit) % 2

    def swap(self, a, even, odd=None):
        odd = even if odd is None else odd
        pairs = []
        for s in range(self.shards):
            for r in range(self.replicas):
                shard, bit = odd if r % 2 else even
                pairs.append((s * self.replicas + r, (s ^ shard) * self.replicas + (r ^ bit)))
        return lax.ppermute(a, AXES, pairs)


def tie(values, others):
    return lax.optimization_barrier((tuple(values), tuple(others)))[0]


def flow(grid, keeps, sends, gots, split):
    rows = sum(k.shape[2] for k in keeps)
    lanes = keeps[0].shape[3]
    ops = 10**4
    after = yield sends
    gots = tie(gots, after)
    two = shape(2, rows, lanes)
    send, keep = call(add_first_kernel, "add_core", [two, two], ops,
                      in_specs=[whole()] * (2 * len(keeps)), out_specs=[whole()] * 2)(*keeps, *gots)
    got = grid.swap(send, (1, 0), (0, SIDE))
    after = yield [send]
    (got,) = tie([got], after)
    one = shape(rows, lanes)
    send, keep = call(add_second_kernel, "add_second", [one, one], ops,
                      in_specs=[whole()] * 2, out_specs=[whole()] * 2)(keep, got)
    got = grid.swap(send, (0, SIDE), (1, 0))
    after = yield [send]
    (got,) = tie([got], after)

    def add(a, b):
        return call(add_kernel, "add", shape(*a.shape), ops, in_specs=[whole()] * 2, out_specs=whole())(a, b)

    if split:
        half = shape(rows // 2, lanes)
        send, keep = call(add_split_kernel, "add_split", [half, half], ops,
                          in_specs=[smem()] + [whole()] * 2, out_specs=[whole()] * 2)(grid.ids, keep, got)
    else:
        send = keep = add(keep, got)
    got = grid.swap(send, (0, SPLIT))
    after = yield [send]
    (got,) = tie([got], after)
    a = add(keep, got)
    for bit in grid.rest[1:]:
        a = add(a, grid.swap(a, (0, bit)))
    got = grid.swap(a, (0, grid.rest[0]))
    after = yield [a]
    (got,) = tie([got], after)
    a = add(a, got)
    if split:
        got = grid.swap(a, (0, SPLIT))
        after = yield [a]
        (got,) = tie([got], after)
        a = call(join_kernel, "join", one, ops, in_specs=[smem()] + [whole()] * 2, out_specs=whole())(grid.ids, a, got)
    b = grid.swap(a, (0, SIDE))
    far = grid.swap(a, (0, CORE))
    after = yield [a]
    (b,) = tie([b], after)
    far_b = grid.swap(b, (0, CORE))
    yield a, b, far, far_b


def local(shards, replicas, tokens, cotangent, lengths, attn_gain, w_query, key_projection,
          value_projection, w_out, mlp_gain, w_gate, w_up, w_down):
    grid = Grid(shards, replicas)
    ids = grid.ids
    count, width = tokens.shape
    rows = w_query.shape[0]
    size = rows // 2
    ff = w_gate.shape[1]
    blocks = ff // 2 // BLOCK
    wide_k = key_projection.shape[1]
    wide = width + 2 * wide_k
    x = tokens.T
    cot = cotangent.T
    cos, sin = tables(count)
    own_down = w_down.T
    padded = -(-rows // LANES) * LANES
    other_one, other_two = grid.swap(attn_gain, (1, 0)), grid.swap(mlp_gain, (1, 0))
    none = jnp.zeros((6, rows), BF)
    gain_rows = jnp.concatenate([attn_gain[None], mlp_gain[None], none, other_one[None], other_two[None], none])
    gain_rows = jnp.pad(gain_rows.astype(F32), ((0, 0), (0, padded - rows)))

    own_qkv, half_qkv = call(
        pack_first_kernel, "pack_first", [shape(rows, wide), shape(size, wide)], 10**6, grid=(1,), limit=60,
        in_specs=[smem(), copied(rows, width), copied(rows, wide_k), copied(rows, wide_k)],
        out_specs=[copied(rows, wide), copied(size, wide)],
    )(ids, w_query, key_projection, value_projection)
    first_qkv = grid.swap(half_qkv, (1, 0))

    tall = [(6 + (-(-width // BLOCK) if b == 0 else 0)) * size for b in range(blocks)]
    (w_gate_,) = tie([w_gate], [half_qkv])
    pack_a, pack_b, pack_c = call(
        pack_kernel, "pack", [shape(t, BLOCK) for t in tall], 10**6, grid=(1,), limit=60,
        in_specs=[smem(), copied(rows, ff), copied(rows, ff), copied(width, ff // 2), copied(rows, width)],
        out_specs=[copied(t, BLOCK) for t in tall],
    )(ids, w_gate_, w_up, own_down, w_out)
    first_a = grid.swap(pack_a, (1, 0))
    (first_qkv,) = tie([first_qkv], [pack_a])
    second_qkv = grid.swap(first_qkv, (0, CORE))

    normed, q, k, v, w_qkv, gains = call(
        qkv_kernel, "qkv",
        [shape(width, count), shape(width, count), shape(wide_k, count), shape(wide_k, count), shape(width, wide),
         shape(width, 8, dtype=F32)],
        2 * count * width * wide, in_specs=[smem()] + [whole()] * 7, out_specs=[whole()] * 6,
    )(ids, x, gain_rows, own_qkv, first_qkv, second_qkv, cos, sin)
    first_b = grid.swap(tie([pack_b], [q])[0], (1, 0))

    group = GROUP * HEAD_SIZE

    def of_group(g):
        block_q = pl.BlockSpec((group, count), lambda i: (g, 0))
        return block_q, pl.BlockSpec((HEAD_SIZE, count), lambda i: (g, 0))

    heads, lse = [], []
    q_ = q
    for g in range(KEY_VALUE_HEADS):
        block_q, block_k = of_group(g)
        o, l = call(
            attend_kernel, "attend", [shape(group, count), shape(8, count, dtype=F32)], 8 * count * count * group,
            grid=(1,), in_specs=[block_q, block_k, block_k], out_specs=[copied(group, count), copied(8, count)], limit=20,
        )(q_, k, v)
        heads.append(o)
        lse.append(l)
        (q_,) = tie([q], [o])
    first_c = grid.swap(tie([pack_c], heads[:1])[0], (1, 0))
    (first_a,) = tie([first_a], heads)
    second_a = grid.swap(first_a, (0, CORE))

    middle, normed_two, w_o, all_heads = call(
        middle_kernel, "middle",
        [shape(width, count, dtype=F32), shape(width, count), shape(width, width), shape(width, count)],
        2 * count * width * width, in_specs=[smem()] + [whole()] * 8, out_specs=[whole()] * 4,
    )(ids, x, *heads, w_out, first_a, second_a, gains)

    scratch = [pltpu.VMEM((width, 4 * BLOCK), BF), pltpu.VMEM((width, 2 * BLOCK), BF), pltpu.VMEM((6 * BLOCK, count), BF)]
    float_act = shape(width, count, dtype=F32)

    def mlp(kernel, b, outs, first, second, more):
        return call(
            functools.partial(kernel, b), "mlp", outs, 18 * count * width * ff // blocks,
            in_specs=[smem()] + [whole()] * (7 + len(more)), out_specs=[whole()] * len(outs),
            scratch=scratch, limit=16, weight=10,
        )(ids, normed_two, cot, w_gate, w_up, own_down, first, second, *more)

    part = (2, 2, 3 * rows, LANES)
    keep_a, send_a, acc, gn = mlp(mlp_one_kernel, 0, [shape(*part)] * 2 + [float_act] * 2, first_a, second_a, [])
    (first_b,) = tie([first_b], [acc])
    second_b = grid.swap(first_b, (0, CORE))
    got_a = grid.swap(send_a, (0, CORE))
    keep_b, send_b, acc, gn = mlp(
        mlp_two_kernel, 1, [shape(*part)] * 2 + [float_act] * 2, first_b, second_b, [acc, gn])
    got_b = grid.swap(send_b, (0, CORE))
    (first_c,) = tie([first_c], [acc])
    second_c = grid.swap(first_c, (0, CORE))
    keep_c, send_c, acc, gn = mlp(
        mlp_two_kernel, 2, [shape(*part)] * 2 + [float_act] * 2, first_c, second_c, [acc, gn])
    got_c = grid.swap(send_c, (0, CORE))
    flows = {"a": flow(grid, [keep_a, keep_b], [send_a, send_b], [got_a, got_b], True)}
    next(flows["a"])
    sums = {}
    state = {"after": [acc]}

    def step(names):
        for name in names:
            sent = flows[name].send(state["after"])
            if len(sent) == 4:
                sums[name] = sent
            else:
                state["after"] = sent

    def then(value):
        return tie([value], state["after"])[0]

    step("a")
    per = -(-(-(-width // LANES)) // 2)
    part_o = (2, 2, -(-per * size // 32) * 32, LANES)
    keep_o, send_o, out, g_mid, g_heads = call(
        between_kernel, "between",
        [shape(*part_o), shape(*part_o), shape(width, count), float_act, shape(width, count)],
        4 * count * width * width, in_specs=[smem()] + [whole()] * 7, out_specs=[whole()] * 5, limit=24, weight=10,
    )(ids, then(cot), acc, gn, middle, gains, all_heads, w_o)
    flows["b"] = flow(grid, [keep_c, keep_o], [send_c, send_o], [got_c, grid.swap(send_o, (0, CORE))], True)
    next(flows["b"])
    state["after"] = [g_heads]

    grads = []
    for g, name in enumerate(('ba', '', 'ba')):
        block_q, block_k = of_group(g)
        out_q, out_k = copied(group, count), copied(HEAD_SIZE, count)
        grads.append(call(
            attend_back_kernel, "attend_back", [shape(group, count), shape(HEAD_SIZE, count), shape(HEAD_SIZE, count)],
            4 * count * count * width, grid=(1,),
            in_specs=[block_q, block_k, block_k, out_q, copied(8, count), block_q] + [copied(HALF, count)] * 2,
            out_specs=[out_q, out_k, out_k],
            scratch=[pltpu.VMEM((HEAD_SIZE, count), F32)] * 2, limit=24, weight=10 if g == 0 else 1,
        )(q, k, v, heads[g], lse[g], then(g_heads), cos, sin))
        state["after"] = [grads[-1][2]]
        step(name)
    grads = [g[i] for i in range(3) for g in grads]

    lanes = -(-wide // (2 * LANES)) * LANES
    part_three = (2, 2, size, lanes)
    keep_d, send_d = call(
        weight_kernel, "weights", [shape(*part_three), shape(*part_three)], 2 * count * width * wide,
        in_specs=[smem()] + [whole()] * 10, out_specs=[whole()] * 2,
    )(ids, then(normed), *grads)
    flows["d"] = flow(grid, [keep_d], [send_d], [grid.swap(send_d, (0, CORE))], False)
    next(flows["d"])
    state["after"] = [send_d]
    step("dab")
    grad_tokens = call(
        tokens_kernel, "grad_tokens", shape(width, count), 2 * count * width * wide,
        in_specs=[whole()] * 13, out_specs=whole(),
    )(then(x), gains, w_qkv, g_mid, *grads)
    state["after"] = [grad_tokens]
    step("dbdadbadbad")
    g_gate, g_up, g_down, partial = call(
        finish_first_kernel, "finish_first",
        [shape(rows, ff, dtype=F32), shape(rows, ff, dtype=F32), shape(width, ff // 2, dtype=F32),
         shape(rows, LANES, dtype=F32)],
        10**7, in_specs=[smem()] + [whole()] * 6, out_specs=[whole()] * 4,
    )(ids, *sums["a"], then(w_gate), w_up)
    g_query, g_key, g_value, g_gain_one = call(
        finish_qkv_kernel, "finish_qkv",
        [shape(rows, width, dtype=F32), shape(rows, wide_k, dtype=F32), shape(rows, wide_k, dtype=F32),
         shape(rows, dtype=F32)],
        10**7, in_specs=[smem()] + [whole()] * 6, out_specs=[whole()] * 4, scratch=[pltpu.VMEM((rows, LANES), F32)],
    )(ids, *sums["d"], tie([own_qkv], [partial])[0], gain_rows)
    state["after"] = [partial]
    step("b")
    piece = pl.BlockSpec((rows, BLOCK), lambda i: (0, (i + 1) * blocks - 1))
    last = pl.BlockSpec((width, BLOCK), lambda i: (0, blocks - 1))
    kept = pl.BlockSpec(memory_space=pl.ANY)
    tall = sums["b"][0].shape
    g_gate, g_up, g_down, g_out, g_gain_two = call(
        finish_last_kernel, "finish_last",
        [shape(rows, ff, dtype=F32), shape(rows, ff, dtype=F32), shape(width, ff // 2, dtype=F32),
         shape(rows, width, dtype=F32), shape(rows, dtype=F32)],
        10**7, grid=(2,),
        in_specs=[smem()] + [copied(*tall)] * 4 + [piece, piece, copied(rows, LANES), copied(16, padded)] + [kept] * 3,
        out_specs=[piece, piece, last, copied(rows, width), copied(rows)],
        scratch=[pltpu.VMEM((rows, LANES), F32)], aliases={9: 0, 10: 1, 11: 2},
    )(ids, *sums["b"], w_gate, w_up, partial, gain_rows, g_gate, g_up, g_down)
    return (
        out.T,
        grad_tokens.T,
        g_gain_one,
        g_query,
        g_key,
        g_value,
        g_out,
        g_gain_two,
        g_gate,
        g_up,
        g_down.T,
    )


def solution(mesh):
    tokens = P(AXES, None)
    split = P("shard", None)
    gain = P("shard")
    return jax.shard_map(
        functools.partial(local, mesh.shape["shard"], mesh.shape["replica"]),
        mesh=mesh,
        in_specs=(tokens, tokens, tokens, gain, split, split, split, split, gain, split, split, split),
        out_specs=(tokens, tokens, gain, split, split, split, split, gain, split, split, split),
        check_vma=False,
    )
```
